32 devices in a mesh: dp: 16 (over z, y, x), mp: 2 (over core).
Axes of the slice: x: 2, y: 2, z: 4, core: 2. Of those that a mesh axis runs over, the one named last changes fastest.
Arguments:
- tokens_in: bfloat16 [65536, 1024], P('dp'), may hold values from -6 to 6
- route_mask: int32 [65536], P('dp'), may hold values from 0 to 1, as said below
- cotangent: bfloat16 [65536, 1024], P('dp'), may hold values from -6 to 6
- w_query: bfloat16 [1024, 1024], P('dp', 'mp'), may hold values from -0.1875 to 0.1875
- w_key: bfloat16 [1024, 1024], P('dp', 'mp'), may hold values from -0.1875 to 0.1875
- w_value: bfloat16 [1024, 1024], P('dp', 'mp'), may hold values from -0.1875 to 0.1875
- w_out: bfloat16 [1024, 1024], P('mp', 'dp'), may hold values from -1 to 1
- w_up: bfloat16 [1024, 4096], P('dp', 'mp'), may hold values from -0.1875 to 0.1875
- w_down: bfloat16 [4096, 1024], P('mp', 'dp'), may hold values from -0.1875 to 0.1875
- gain_attn: bfloat16 [1024], P('dp'), may hold values from 0.099609375 to 1.8984375
- gain_mlp: bfloat16 [1024], P('dp'), may hold values from 0.099609375 to 1.8984375
- router: bfloat16 [1024], P('dp'), may hold values from -0.1875 to 0.1875
Outputs:
- block_out: bfloat16 [65536, 1024], P('dp')
- input_grad: bfloat16 [65536, 1024], P('dp')
- grad_query: float32 [1024, 1024], P('dp', 'mp')
- grad_key: float32 [1024, 1024], P('dp', 'mp')
- grad_value: float32 [1024, 1024], P('dp', 'mp')
- grad_out: float32 [1024, 1024], P('mp', 'dp')
- grad_up: float32 [1024, 4096], P('dp', 'mp')
- grad_down: float32 [4096, 1024], P('mp', 'dp')
- grad_gain_attn: float32 [1024], P('dp')
- grad_gain_mlp: float32 [1024], P('dp')
- grad_router: float32 [1024], P('dp')
- routed_share: float32 [], replicated
- gate_mean: float32 [], replicated
The draws below stay inside these ranges and needn't reach their ends.
Inputs may be any that keep to these rules, and one draw needn't show every extreme that they name: `route_mask`: sequence s holds tokens s * 2048 to (s + 1) * 2048 - 1. Every sequence has 1 to 256 routed tokens, and some sequence has exactly 256. For every i below 16, the routed counts of sequence 2 i and of sequence 2 j + 1, where j is i with the highest bit of 15 flipped, add up to at most 320, exactly 320 for some i.
All inputs are finite; a program needn't handle non-finite values.
Results may differ from the reference program's by a relative error of at most 0.018.
Values may be sent and summed in bfloat16 or wider, within the bound.
No kernel may reach another device: no remote copies, remote signals or barrier semaphores. Data moves between devices by JAX's collectives and lax.ppermute only.
A program may use at most 192 MiB of HBM per device.

```python
import jax
import jax.numpy as jnp
from jax import lax

HEADS = 16
HD = 64
D = 1024
FF = 4096
LEN = 2048
CAP = 256
PAIR_CAP = 320
SEQS = 32
TOKENS = 65536


def draw_route_mask(key, part):
    key = jax.random.fold_in(key, 11)
    devices = SEQS // 2
    half_count = devices // 2
    index = jnp.arange(devices)
    spread = CAP // 16 + 1
    first_key, second_key, order_key = jax.random.split(key, 3)
    rising = CAP // 3 + (CAP - CAP // 3) * index // (devices - 1)
    first = jnp.minimum(CAP, rising + jax.random.randint(first_key, (devices,), 0, spread))
    jitter = jax.random.randint(second_key, (devices,), 0, spread) * (index > 0).astype(jnp.int32)
    partner = jnp.bitwise_xor(index, half_count)
    second = PAIR_CAP - first[partner] - jitter
    counts = jnp.stack([first, second], axis=1).reshape(SEQS)
    order_keys = jax.random.split(order_key, SEQS)
    orders = jax.vmap(lambda each_key: jax.random.permutation(each_key, LEN))(order_keys)
    ranks = jnp.argsort(orders, axis=1)
    return (ranks < counts[:, None]).astype(jnp.int32).reshape(SEQS * LEN)


def steps_of(key, dims, shards, least, largest):
    def one(dim, parts):
        heights = jax.random.uniform(jax.random.fold_in(jax.random.fold_in(key, 6), dim), (parts,), jnp.float32, least / len(shards), largest / len(shards))
        return jnp.repeat(jnp.exp(heights), dims[dim] // parts).reshape((-1,) + (1,) * (len(dims) - dim - 1))

    factor_of = one(*shards[0])
    for cut in shards[1:]:
        factor_of = factor_of * one(*cut)
    return factor_of


def gaussian(key, extent, scale, reach, shards=(), kind=jnp.bfloat16):
    entries = scale * jax.random.normal(key, extent, jnp.float32)
    if shards:
        entries = entries * steps_of(key, extent, shards, -0.22, 0.18)
    return jnp.clip(entries, -reach, reach).astype(kind)


def setup_inputs(seed: int = 0) -> dict:
    key_list = jax.random.split(jax.random.key(seed), 13)
    tokens_in = gaussian(key_list[0], (TOKENS, D), 1.0, 6.0, ((0, 16),))
    route_mask = draw_route_mask(jax.random.fold_in(key_list[12], 71), 0)
    cotangent = gaussian(key_list[2], (TOKENS, D), 1.0, 6.0, ((0, 16),))
    w_query = gaussian(key_list[3], (D, D), D ** -0.5, 0.1875, ((0, 16), (1, 2)))
    w_key = gaussian(key_list[4], (D, D), D ** -0.5, 0.1875, ((0, 16), (1, 2)))
    w_value = gaussian(key_list[5], (D, D), D ** -0.5, 0.1875, ((0, 16), (1, 2)))
    w_out = gaussian(key_list[6], (D, D), (D // 32) ** -0.5, 1.0, ((0, 2), (1, 16)))
    w_up = gaussian(key_list[7], (D, FF), D ** -0.5, 0.1875, ((0, 16), (1, 2)))
    w_down = gaussian(key_list[8], (FF, D), (FF // 4) ** -0.5, 0.1875, ((0, 2), (1, 16)))
    gain_attn = jnp.clip(1.0 + 0.18 * jax.random.normal(key_list[9], (D,), jnp.float32), 0.099609375, 1.8984375).astype(jnp.bfloat16)
    gain_mlp = jnp.clip(1.0 + 0.18 * jax.random.normal(key_list[10], (D,), jnp.float32), 0.099609375, 1.8984375).astype(jnp.bfloat16)
    router = gaussian(key_list[11], (D,), D ** -0.5, 0.1875, ((0, 16),))
    return dict(tokens_in=tokens_in, route_mask=route_mask, cotangent=cotangent, w_query=w_query, w_key=w_key, w_value=w_value, w_out=w_out, w_up=w_up, w_down=w_down, gain_attn=gain_attn, gain_mlp=gain_mlp, router=router)


epsilon = 1e-06
negative = -1e+30
highest = lax.Precision.HIGHEST

@jax.custom_vjp
def low(v):
    return lax.optimization_barrier(v.astype(jnp.bfloat16)).astype(jnp.float32)

@jax.custom_vjp
def low_back(v):
    return v

def low_keep(v):
    return (low(v), None)

def low_pass(kept, grad):
    return (grad,)

def back_keep(v):
    return (v, None)

def back_low(kept, grad):
    return (low(grad),)
low.defvjp(low_keep, low_pass)
low_back.defvjp(back_keep, back_low)

def rms_norm(values, gain_row):
    return values * lax.rsqrt(lax.optimization_barrier(jnp.mean(values * values, axis=-1, keepdims=True)) + epsilon) * gain_row

def block_rows(routed, allowed, params):
    w_query, w_key, w_value, w_out, w_up, w_down, gain_attn, gain_mlp, router = params
    row_count = routed.shape[0]
    score_scale = HD ** (-0.5)
    gate_value = jax.nn.sigmoid(jnp.dot(routed, router, precision=highest))
    normed = low(rms_norm(routed, gain_attn))

    def split_heads(weight_matrix):
        projected = low(low_back(jnp.dot(normed, weight_matrix, precision=highest)))
        return projected.reshape(row_count, HEADS, HD)
    queries = split_heads(w_query)
    key_heads = split_heads(w_key)
    value_heads = split_heads(w_value)
    scores = low_back(jnp.einsum('qhe,khe->hqk', queries, key_heads, precision=highest) * score_scale)
    scores = jnp.where(allowed[None], scores, negative)
    probability = jax.nn.softmax(scores, axis=-1)
    attended = low(low_back(jnp.einsum('hqk,khe->qhe', low(probability), value_heads, precision=highest)))
    attention = low_back(jnp.dot(attended.reshape(row_count, HEADS * HD), w_out, precision=highest))
    residual = routed + attention
    normed_two = low(rms_norm(residual, gain_mlp))
    hidden = low_back(jnp.dot(normed_two, w_up, precision=highest))
    active = low(jax.nn.gelu(hidden))
    feed_out = low_back(jnp.dot(active, w_down, precision=highest))
    return routed + gate_value[:, None] * (attention + feed_out)

def sequence_out(sequence, selected, params):
    routed_count = jnp.sum(selected)
    slot_index = jnp.nonzero(selected, size=CAP, fill_value=LEN)[0].astype(jnp.int32)
    routed = jnp.take(sequence, slot_index, axis=0, mode='fill', fill_value=0.0)
    position = jnp.arange(CAP)
    usable = position < routed_count
    allowed = (position[None, :] <= position[:, None]) & usable[None, :]
    result_rows = block_rows(routed, allowed, params)
    return sequence.at[slot_index].set(result_rows, mode='drop')

def reference(tokens_in, route_mask, cotangent, w_query, w_key, w_value, w_out, w_up, w_down, gain_attn, gain_mlp, router):
    params = (w_query.astype(jnp.float32), w_key.astype(jnp.float32), w_value.astype(jnp.float32), w_out.astype(jnp.float32), w_up.astype(jnp.float32), w_down.astype(jnp.float32), gain_attn.astype(jnp.float32), gain_mlp.astype(jnp.float32), router.astype(jnp.float32))
    inputs = tokens_in.astype(jnp.float32)
    selections = route_mask.reshape(SEQS, LEN)

    def forward(values, weight_set):
        sequences = values.reshape(SEQS, LEN, D)

        def one_sequence(item_pair):
            return sequence_out(item_pair[0], item_pair[1], weight_set)
        return lax.map(jax.checkpoint(one_sequence), (sequences, selections)).reshape(TOKENS, D)
    output, pullback = jax.vjp(forward, inputs, params)
    d_inputs, d_params = pullback(cotangent.astype(jnp.float32))
    gate_all = jax.nn.sigmoid(jnp.dot(inputs, params[8], precision=highest))
    routed_flag = route_mask.astype(jnp.float32)
    routed_total = jnp.sum(routed_flag)
    return (output.astype(jnp.bfloat16), d_inputs.astype(jnp.bfloat16), d_params[0], d_params[1], d_params[2], d_params[3], d_params[4], d_params[5], d_params[6], d_params[7], d_params[8], routed_total / TOKENS, jnp.sum(gate_all * routed_flag) / routed_total)
```

```python
import functools
import jax
import jax.numpy as jnp
from jax import lax
from jax.experimental import pallas as pl
from jax.experimental.pallas import tpu as pltpu
from jax.sharding import PartitionSpec as P

HD = 64
LEN = 2048
CAP = 256

epsilon = 1e-06
negative = -1e30
BF = jnp.bfloat16
F32 = jnp.float32


def matmul(left_side, right_side):
    return jnp.dot(left_side, right_side, preferred_element_type=F32)


def matmul_nt(left_side, right_side):
    return lax.dot_general(left_side, right_side, (((1,), (1,)), ((), ())), preferred_element_type=F32)


def bit_orders(n):
    bits = n.bit_length() - 1
    if bits == 4:
        x, y, z1, z2 = 1, 2, 4, 8
        first = ((z2, z1, x, y), (z2, z1, y, x))
        second = ((x, z2, z1, y), (y, z2, z1, x))
        return (first, second, second)
    down = tuple(1 << b for b in reversed(range(bits)))
    return ((down, down),) * 3


def pairs(n, one, two):
    return [(d * 2 + c, (d ^ (one, two)[c]) * 2 + c) for d in range(n) for c in range(2)]


def block_ids(n, orders):
    me = lax.axis_index("dp")
    core = lax.axis_index("mp")
    tables = []
    for order in orders:
        table = [0]
        for bit in order:
            table = table + [t ^ bit for t in table]
        tables.append(table)
    return me ^ jnp.where(core == 0, jnp.array(tables[0], jnp.int32), jnp.array(tables[1], jnp.int32))


def gather(shard, n, orders):
    held = shard
    for one, two in zip(*orders):
        got = lax.ppermute(held, ("dp", "mp"), pairs(n, one, two))
        held = jnp.concatenate([held, got], axis=0)
    return held


def scatter_sum(ordered, n, orders):
    held = ordered
    steps = list(zip(*orders))[::-1]
    for at, (one, two) in enumerate(steps):
        half = held.shape[0] // 2
        got = lax.ppermute(held[half:], ("dp", "mp"), pairs(n, one, two))
        held = held[:half].astype(F32) + got.astype(F32)
        if at < len(steps) - 1:
            held = held.astype(BF)
    return held


def reorder_kernel(ids_ref, in_ref, out_ref):
    out_ref[...] = in_ref[...].astype(out_ref.dtype)


def reorder(array, ids, n, inverse):
    rows, width = array.shape
    step = rows // n
    if step % 16:
        blocks = array.reshape(n, step, width)
        if inverse:
            blocks = jnp.zeros_like(blocks).at[ids].set(blocks)
        else:
            blocks = blocks[ids]
        return blocks.reshape(rows, width).astype(BF)
    here = lambda i, ids_ref: (i, 0)
    there = lambda i, ids_ref: (ids_ref[i], 0)
    return pl.pallas_call(
        reorder_kernel,
        grid_spec=pltpu.PrefetchScalarGridSpec(
            num_scalar_prefetch=1,
            grid=(n,),
            in_specs=[pl.BlockSpec((step, width), here if inverse else there)],
            out_specs=pl.BlockSpec((step, width), there if inverse else here),
        ),
        out_shape=jax.ShapeDtypeStruct((rows, width), BF),
        cost_estimate=pl.CostEstimate(flops=0, bytes_accessed=4 * rows * width, transcendentals=0),
    )(ids, array)


def compact(sequence, selected):
    slot_index = jnp.nonzero(selected, size=CAP, fill_value=LEN)[0].astype(jnp.int32)
    picked = jnp.take(sequence, slot_index, axis=0, mode="fill", fill_value=0)
    return (picked, slot_index)


def swap_sum(part):
    low = part.astype(BF)
    other = lax.ppermute(low, "mp", [(0, 1), (1, 0)])
    return low.astype(F32) + other.astype(F32)


def body(
    tokens_in,
    route_mask,
    cotangent,
    w_query,
    w_key,
    w_value,
    w_out,
    w_up,
    w_down,
    gain_attn,
    gain_mlp,
    router,
):
    n = lax.axis_size("dp")
    orders = bit_orders(n)
    ids = [block_ids(n, o) for o in orders]
    mine = w_query.shape[0]
    heads_width = w_query.shape[1]
    width = tokens_in.shape[1]
    seqs = tokens_in.shape[0] // LEN
    extras = jnp.concatenate(
        [gain_attn[:, None], gain_mlp[:, None], router[:, None], jnp.zeros((mine, 125), BF)], axis=1
    )
    shard_attn = jnp.concatenate([w_query, w_key, w_value, w_out.T, extras], axis=1)
    full_attn = reorder(gather(shard_attn, n, orders[0]), ids[0], n, True)
    full_up = reorder(gather(w_up, n, orders[1]), ids[1], n, True)
    full_down = reorder(gather(w_down.T, n, orders[2]), ids[2], n, True)
    w = heads_width
    w_qkv = full_attn[:, : 3 * w]
    w_out_t = full_attn[:, 3 * w : 4 * w]
    vectors = full_attn[:, 4 * w :]
    gain_one = vectors[:, 0].astype(F32)
    gain_two = vectors[:, 1].astype(F32)
    router_all = vectors[:, 2]

    sequences = tokens_in.reshape(seqs, LEN, width)
    selection = route_mask.reshape(seqs, LEN)
    upstream_all = cotangent.reshape(seqs, LEN, width)
    picked = [compact(sequences[s], selection[s]) for s in range(seqs)]
    slots = [p[1] for p in picked]
    routed = jnp.concatenate([p[0] for p in picked], axis=0)
    upstream_rows = jnp.concatenate(
        [jnp.take(upstream_all[s], slots[s], axis=0, mode="fill", fill_value=0) for s in range(seqs)], axis=0
    )
    counts = jnp.sum(selection, axis=1)
    position = jnp.arange(CAP)
    usable = position[None, :] < counts[:, None]
    allowed = (position[None, :] <= position[:, None])[None] & usable[:, None, :]
    rows = seqs * CAP
    local_heads = w // HD
    scale = HD ** (-0.5)

    inputs = routed.astype(F32)
    gate = jax.nn.sigmoid(matmul(routed, router_all))
    inverse_one = lax.rsqrt(jnp.mean(inputs * inputs, axis=-1, keepdims=True) + epsilon)
    normal_one = inputs * inverse_one
    normed = (normal_one * gain_one).astype(BF)
    qkv = matmul(normed, w_qkv).astype(BF).reshape(seqs, CAP, 3, local_heads, HD)
    queries, key_heads, value_heads = qkv[:, :, 0], qkv[:, :, 1], qkv[:, :, 2]
    scores = jnp.einsum("sqhe,skhe->shqk", queries, key_heads, preferred_element_type=F32) * scale
    scores = jnp.where(allowed[:, None], scores, negative)
    probability = jax.nn.softmax(scores, axis=-1)
    probability_low = probability.astype(BF)
    attended = jnp.einsum("shqk,skhe->sqhe", probability_low, value_heads, preferred_element_type=F32)
    attended = attended.astype(BF).reshape(rows, w)
    attention = swap_sum(matmul_nt(attended, w_out_t))
    residual = inputs + attention
    inverse_two = lax.rsqrt(jnp.mean(residual * residual, axis=-1, keepdims=True) + epsilon)
    normal_two = residual * inverse_two
    normed_two = (normal_two * gain_two).astype(BF)
    hidden = matmul(normed_two, full_up)
    active, gelu_back = jax.vjp(jax.nn.gelu, hidden)
    active = active.astype(BF)
    upstream = upstream_rows.astype(F32)
    d_branch = gate[:, None] * upstream
    d_feed = d_branch.astype(BF)
    grad_down = matmul(d_feed.T, active).astype(BF)
    sum_down = scatter_sum(reorder(grad_down, ids[2], n, False), n, orders[2])

    d_active = matmul(d_feed, full_down)
    d_hidden = gelu_back(d_active)[0].astype(BF)
    grad_up = matmul(normed_two.T, d_hidden).astype(BF)
    sum_up = scatter_sum(reorder(grad_up, ids[1], n, False), n, orders[1])
    d_normed_two = swap_sum(matmul_nt(d_hidden, full_up))
    scaled = d_normed_two * gain_two
    d_inner = inverse_two * (scaled - normal_two * jnp.mean(scaled * normal_two, axis=-1, keepdims=True))
    grad_gain_two = jnp.sum(d_normed_two * normal_two, axis=0)
    d_attention = (d_branch + d_inner).astype(BF)
    grad_out = matmul(d_attention.T, attended).astype(BF)
    d_attended = matmul(d_attention, w_out_t).astype(BF).reshape(seqs, CAP, local_heads, HD)
    d_probability = jnp.einsum("sqhe,skhe->shqk", d_attended, value_heads, preferred_element_type=F32)
    d_values = jnp.einsum("shqk,sqhe->skhe", probability_low, d_attended, preferred_element_type=F32)
    d_scores = probability * (d_probability - jnp.sum(probability * d_probability, axis=-1, keepdims=True))
    d_scores = d_scores.astype(BF)
    d_queries = jnp.einsum("shqk,skhe->sqhe", d_scores, key_heads, preferred_element_type=F32) * scale
    d_keys = jnp.einsum("shqk,sqhe->skhe", d_scores, queries, preferred_element_type=F32) * scale
    d_qkv = jnp.concatenate(
        [d_queries.astype(BF).reshape(rows, w), d_keys.astype(BF).reshape(rows, w), d_values.astype(BF).reshape(rows, w)],
        axis=1,
    )
    grad_qkv = matmul(normed.T, d_qkv).astype(BF)
    sum_attn = scatter_sum(
        reorder(jnp.concatenate([grad_qkv, grad_out], axis=1), ids[0], n, False), n, orders[0]
    )
    d_normed = swap_sum(matmul_nt(d_qkv, w_qkv))
    scaled = d_normed * gain_one
    d_norm_input = inverse_one * (scaled - normal_one * jnp.mean(scaled * normal_one, axis=-1, keepdims=True))
    grad_gain_one = jnp.sum(d_normed * normal_one, axis=0)

    feed_out = swap_sum(matmul_nt(active, full_down))
    branch = attention + feed_out
    output = (inputs + gate[:, None] * branch).astype(BF)
    d_logit = jnp.sum(upstream * branch, axis=-1) * gate * (1.0 - gate)
    d_router = jnp.sum(d_logit[:, None] * inputs, axis=0)
    d_rows = upstream + d_inner + d_logit[:, None] * router_all.astype(F32) + d_norm_input
    d_rows = d_rows.astype(BF)

    usable_rows = usable.reshape(-1)
    scalars = jnp.stack([jnp.sum(counts).astype(F32), jnp.sum(jnp.where(usable_rows, gate, 0.0))])
    small = jnp.concatenate(
        [
            grad_gain_one.reshape(n, mine),
            grad_gain_two.reshape(n, mine),
            d_router.reshape(n, mine),
            jnp.broadcast_to(scalars, (n, 2)),
        ],
        axis=1,
    )
    small = lax.all_to_all(small, "dp", 0, 0, tiled=True)
    small = jnp.sum(small, axis=0)
    block_out = jnp.stack(
        [sequences[s].at[slots[s]].set(output[s * CAP : (s + 1) * CAP], mode="drop") for s in range(seqs)]
    ).reshape(-1, width)
    input_grad = jnp.stack(
        [upstream_all[s].at[slots[s]].set(d_rows[s * CAP : (s + 1) * CAP], mode="drop") for s in range(seqs)]
    ).reshape(-1, width)
    token_total = tokens_in.shape[0] * n
    return (
        block_out,
        input_grad,
        sum_attn[:, :w],
        sum_attn[:, w : 2 * w],
        sum_attn[:, 2 * w : 3 * w],
        sum_attn[:, 3 * w :].T,
        sum_up,
        sum_down.T,
        small[:mine],
        small[mine : 2 * mine],
        small[2 * mine : 3 * mine],
        small[3 * mine] / token_total,
        small[3 * mine + 1] / small[3 * mine],
    )


def solution(mesh):
    return jax.shard_map(
        body,
        mesh=mesh,
        in_specs=(
            P("dp", None),
            P("dp"),
            P("dp", None),
            P("dp", "mp"),
            P("dp", "mp"),
            P("dp", "mp"),
            P("mp", "dp"),
            P("dp", "mp"),
            P("mp", "dp"),
            P("dp"),
            P("dp"),
            P("dp"),
        ),
        out_specs=(
            P("dp", None),
            P("dp", None),
            P("dp", "mp"),
            P("dp", "mp"),
            P("dp", "mp"),
            P("mp", "dp"),
            P("dp", "mp"),
            P("mp", "dp"),
            P("dp"),
            P("dp"),
            P("dp"),
            P(),
            P(),
        ),
        check_vma=False,
    )
```

```python
import jax
import jax.numpy as jnp
from jax import lax
from jax.experimental import pallas as pl
from jax.experimental.pallas import tpu as pltpu
from jax.sharding import PartitionSpec as P

HD = 64
LEN = 2048
CAP = 256
LANE = 128
EXTRA = 128
MIB = 1 << 20
COST = pl.CostEstimate(flops=8000000000, bytes_accessed=24000000, transcendentals=0)

epsilon = 1e-06
negative = -1e30
BF = jnp.bfloat16
F32 = jnp.float32
SM = pl.BlockSpec(memory_space=pltpu.SMEM)
HB = pl.BlockSpec(memory_space=pltpu.HBM)


def nn(a, b):
    return jnp.dot(a, b, preferred_element_type=F32)


def nt(a, b):
    return lax.dot_general(a, b, (((1,), (1,)), ((), ())), preferred_element_type=F32)


def tn(a, b):
    return lax.dot_general(a, b, (((0,), (0,)), ((), ())), preferred_element_type=F32)


def sds(shape, dtype):
    return jax.ShapeDtypeStruct(shape, dtype)


def color_orders(n):
    bits = n.bit_length() - 1
    if bits == 4:
        x, y, z1, z2 = 1, 2, 4, 8
        return (((z2, y, z1, x), (z2, z1, x, y)), ((z2, x, y, z1), (z2, x, y, z1)))
    down = tuple(1 << b for b in reversed(range(bits)))
    return ((down, down), (down, down))


def bit_sum(n, index, source, target):
    total = jnp.zeros((n,), jnp.int32)
    for one, two in zip(source, target):
        total = total | jnp.where((index & one) != 0, two, 0)
    return total


def spots(orders):
    return [1 << k for k in range(len(orders[0]))]


def owners(n, orders):
    p = jnp.arange(n, dtype=jnp.int32)
    one, two = (bit_sum(n, p, spots(orders), o) for o in orders)
    return lax.axis_index("dp") ^ jnp.where(lax.axis_index("mp") == 0, one, two)


def places(n, orders):
    d = jnp.arange(n, dtype=jnp.int32) ^ lax.axis_index("dp")
    one, two = (bit_sum(n, d, o, spots(orders)) for o in orders)
    return jnp.where(lax.axis_index("mp") == 0, one, two)


def hop(array, n, one, two):
    pairs = [(d * 2 + c, (d ^ (one, two)[c]) * 2 + c) for d in range(n) for c in range(2)]
    return lax.ppermute(array, ("dp", "mp"), pairs)


def other_core(array):
    return lax.ppermute(array, "mp", [(0, 1), (1, 0)])


def split_of(width):
    return -(-width * 2 // (3 * LANE)) * LANE


class Gather:
    def __init__(self, shard, n):
        self.n = n
        self.orders = color_orders(n)
        self.steps = len(self.orders[0][0])
        self.at = 0
        self.width = shard.shape[1]
        self.cut = split_of(self.width)
        self.held = [shard]
        self.got = None

    def begin(self):
        k = self.at
        if k == 0:
            one, two = self.orders[0][0][0], self.orders[0][1][0]
            self.got = [hop(self.held[0], self.n, one, two)]
        else:
            self.got = [hop(h, self.n, o[0][k], o[1][k]) for h, o in zip(self.held, self.orders)]
        self.at += 1
        return self.got

    def end(self):
        if self.at == self.steps:
            return
        if self.at == 1:
            both = jnp.concatenate([self.held[0], self.got[0]], axis=0)
            self.held = [both[:, : self.cut], both[:, self.cut :]]
        else:
            self.held = [jnp.concatenate([h, g], axis=0) for h, g in zip(self.held, self.got)]

    def result(self):
        n = self.n
        ids = jnp.stack([owners(n, o) for o in self.orders])
        halves = [self.held[0], self.got[0], self.held[1], self.got[1]]
        rows = 2 * self.held[0].shape[0]
        if (rows // n) % 16:
            out = []
            for at, (h, g) in enumerate(zip(self.held, self.got)):
                blocks = jnp.concatenate([h, g], axis=0).reshape(n, rows // n, -1)
                blocks = blocks[places(n, self.orders[at])].reshape(rows, -1)
                out += [blocks[: rows // 2], blocks[rows // 2 :]]
            return jnp.zeros((2, 2), jnp.int32) + jnp.arange(2, dtype=jnp.int32), out
        return ids, halves


class Scatter:
    def __init__(self, keep, send, n):
        self.n = n
        self.orders = color_orders(n)
        self.steps = len(self.orders[0][0])
        self.at = self.steps
        self.keep, self.send = keep, send

    def ops(self):
        return self.send

    def begin(self):
        k = self.at - 1
        if len(self.send) == 1:
            one, two = self.orders[0][0][0], self.orders[0][1][0]
            self.got = [hop(self.send[0], self.n, one, two)]
        else:
            self.got = [hop(s, self.n, o[0][k], o[1][k]) for s, o in zip(self.send, self.orders)]
        self.at -= 1
        return self.got

    def end(self):
        total = [k.astype(F32) + g.astype(F32) for k, g in zip(self.keep, self.got)]
        if self.at == 0:
            self.keep, self.send = total, []
            return
        half = total[0].shape[0] // 2
        keep = [t[:half].astype(BF) for t in total]
        send = [t[half:].astype(BF) for t in total]
        if self.at == 1:
            keep = [jnp.concatenate(keep, axis=1)]
            send = [jnp.concatenate(send, axis=1)]
        self.keep, self.send = keep, send

    def result(self):
        return self.keep[0]


def tie(values, tokens):
    if not tokens:
        return list(values)
    out = lax.optimization_barrier(tuple(values) + tuple(tokens))
    return list(out[: len(values)])


def pick_kernel(mask_ref, x_ref, c_ref, r_ref, g_ref, slot_ref, sel):
    groups = mask_ref.shape[1]
    flag = mask_ref[0].astype(F32)
    up = lax.broadcasted_iota(jnp.int32, (LANE, LANE), 0) <= lax.broadcasted_iota(jnp.int32, (LANE, LANE), 1)
    within = nn(flag, up.astype(F32))
    total = jnp.broadcast_to(within[:, LANE - 1 :], (groups, LANE))
    low = lax.broadcasted_iota(jnp.int32, (groups, groups), 1) < lax.broadcasted_iota(
        jnp.int32, (groups, groups), 0
    )
    rank = within + nn(low.astype(F32), total) - 1.0
    slot = jnp.where(flag > 0, rank, -1.0)
    place = lax.broadcasted_iota(jnp.int32, (CAP, LANE), 0).astype(F32)
    for at in range(groups):
        slot_ref[at] = slot[at : at + 1]
        sel[:, at * LANE : (at + 1) * LANE] = jnp.where(place == slot[at : at + 1], 1.0, 0.0).astype(BF)
    r_ref[...] = nn(sel[...], x_ref[...]).astype(BF)
    g_ref[...] = nn(sel[...], c_ref[...]).astype(BF)


def pick(mask, tokens, cotangent, seqs):
    width = tokens.shape[1]
    groups = LEN // LANE
    return pl.pallas_call(
        pick_kernel,
        grid=(seqs,),
        in_specs=[
            pl.BlockSpec((1, groups, LANE), lambda s: (s, 0, 0)),
            pl.BlockSpec((LEN, width), lambda s: (s, 0)),
            pl.BlockSpec((LEN, width), lambda s: (s, 0)),
        ],
        out_specs=[
            pl.BlockSpec((CAP, width), lambda s: (s, 0)),
            pl.BlockSpec((CAP, width), lambda s: (s, 0)),
            pl.BlockSpec((groups, 1, LANE), lambda s: (s, 0, 0)),
        ],
        out_shape=[
            sds((seqs * CAP, width), BF),
            sds((seqs * CAP, width), BF),
            sds((seqs * groups, 1, LANE), F32),
        ],
        scratch_shapes=[pltpu.VMEM((CAP, LEN), BF)],
        compiler_params=pltpu.CompilerParams(vmem_limit_bytes=44 * MIB),
        cost_estimate=COST,
        name="pick",
    )(mask.reshape(seqs, groups, LANE), tokens, cotangent)


class Mover:
    def __init__(self, sem):
        self.sem = sem
        self.used = 0
        self.out = []

    def start(self, src, dst):
        copy = pltpu.make_async_copy(src, dst, self.sem.at[self.used])
        self.used += 1
        copy.start()
        return copy

    def fetch(self, pairs):
        return [self.start(src, dst) for src, dst in pairs]

    def put(self, src, dst):
        self.out.append(self.start(src, dst))

    def weights(self, ids_ref, halves, dst):
        blocks = ids_ref.shape[1]
        rows = dst.shape[0] // blocks
        copies = []
        col = 0
        for piece in range(2):
            width = halves[2 * piece].shape[1]
            for at in range(blocks):
                src = halves[2 * piece + at // (blocks // 2)]
                from_row = (at % (blocks // 2)) * rows
                to_row = pl.multiple_of(ids_ref[piece, at] * rows, rows)
                copies.append(
                    self.start(src.at[pl.ds(from_row, rows), :], dst.at[pl.ds(to_row, rows), pl.ds(col, width)])
                )
            col += width
        return copies

    def block(self, place, blocks, src, keep, send):
        rows = src.shape[0]
        at = self.sem.at[self.used]
        self.used += 1

        @pl.when(place < blocks // 2)
        def _():
            row = pl.multiple_of(place * rows, rows)
            pltpu.make_async_copy(src, keep.at[pl.ds(row, rows), :], at).start()

        @pl.when(place >= blocks // 2)
        def _():
            row = pl.multiple_of((place - blocks // 2) * rows, rows)
            pltpu.make_async_copy(src, send.at[pl.ds(row, rows), :], at).start()

        self.out.append(pltpu.make_async_copy(src, keep.at[pl.ds(0, rows), :], at))

    def finish(self):
        for copy in self.out:
            copy.wait()


def wait(copies):
    for copy in copies:
        copy.wait()


def like(shape, dtype=BF):
    return pltpu.VMEM(shape, dtype)


def hbm_call(kernel, out_shape, scalars, args, scratch, copies, name, limit):
    return pl.pallas_call(
        kernel,
        out_shape=out_shape,
        in_specs=[SM] * len(scalars) + [HB] * len(args),
        out_specs=[HB] * len(out_shape),
        scratch_shapes=list(scratch) + [pltpu.SemaphoreType.DMA((copies,))],
        compiler_params=pltpu.CompilerParams(vmem_limit_bytes=limit * MIB),
        cost_estimate=COST,
        name=name,
    )(*scalars, *args)


def softmax(queries, keys, allowed):
    scores = nt(queries, keys) * (HD**-0.5)
    scores = jnp.where(allowed, scores, negative)
    raised = jnp.exp(scores - jnp.max(scores, axis=-1, keepdims=True))
    return raised / jnp.sum(raised, axis=-1, keepdims=True)


def allowed_slots(count):
    row = lax.broadcasted_iota(jnp.int32, (CAP, CAP), 0)
    col = lax.broadcasted_iota(jnp.int32, (CAP, CAP), 1)
    return (col <= row) & (col < count)


def attn_fwd_kernel(
    ids, count_ref, r_hbm, s0, s1, s2, s3,
    n1_hbm, qkv_hbm, o_hbm, part_hbm, gate_hbm, vec_hbm, p_hbm,
    r, weights, n1, qkv, o, part, gate, vec, prob, sem,
):
    move = Mover(sem)
    rows_in = move.fetch([(r_hbm, r)])
    copies = move.weights(ids, (s0, s1, s2, s3), weights)
    w = o.shape[1]
    seqs = r.shape[0] // CAP
    wait(rows_in)
    inputs = r[...].astype(F32)
    normal = inputs * lax.rsqrt(jnp.mean(inputs * inputs, axis=-1, keepdims=True) + epsilon)
    wait(copies)
    vectors = weights[:, 4 * w :].astype(F32).T[:8]
    vec[...] = vectors
    move.put(vec, vec_hbm)
    n1[...] = (normal * vectors[0:1]).astype(BF)
    move.put(n1, n1_hbm)
    logit = jnp.sum(inputs * vectors[2:3], axis=-1, keepdims=True)
    gate[...] = jnp.broadcast_to(jax.nn.sigmoid(logit), gate.shape)
    move.put(gate, gate_hbm)
    qkv[...] = nn(n1[...], weights[:, : 3 * w]).astype(BF)
    move.put(qkv, qkv_hbm)
    first = lax.broadcasted_iota(jnp.int32, (CAP, 2 * HD), 1) < HD
    pairs = w // (2 * HD)
    for s in range(seqs):
        allowed = allowed_slots(count_ref[s])
        rows = slice(s * CAP, (s + 1) * CAP)
        for pair in range(pairs):
            at = pair * 2 * HD
            q = qkv[rows, at : at + 2 * HD]
            k = qkv[rows, w + at : w + at + 2 * HD]
            v = qkv[rows, 2 * w + at : 2 * w + at + 2 * HD]
            zero = jnp.zeros_like(q)
            one = softmax(jnp.where(first, q, zero), k, allowed)
            two = softmax(jnp.where(first, zero, q), k, allowed)
            head = 2 * (s * pairs + pair)
            prob[head] = one
            prob[head + 1] = two
            o[rows, at : at + 2 * HD] = jnp.where(first, nn(one.astype(BF), v), nn(two.astype(BF), v)).astype(BF)
        half = pl.ds(2 * s * pairs, 2 * pairs)
        move.put(prob.at[half], p_hbm.at[half])
    move.put(o, o_hbm)
    part[...] = nt(o[...], weights[:, 3 * w : 4 * w]).astype(BF)
    move.put(part, part_hbm)
    move.finish()


def attn_fwd(source, counts, routed, w):
    ids, halves = source
    rows, width = routed.shape
    heads = rows // CAP * w // HD
    outs = [
        ((rows, width), BF), ((rows, 3 * w), BF), ((rows, w), BF), ((rows, width), BF),
        ((rows, LANE), F32), ((8, width), F32), ((heads, CAP, CAP), F32),
    ]
    return hbm_call(
        attn_fwd_kernel,
        [sds(*o) for o in outs],
        (ids, counts),
        (routed, *halves),
        [like((rows, width)), like((width, 4 * w + EXTRA))] + [like(*o) for o in outs],
        2 * ids.shape[1] + 16,
        "attn_fwd",
        36,
    )


def grad_tiles(move, pos, tile, at, col, stage, keep, send, piece):
    blocks = pos.shape[1]
    rows = stage.shape[0] // blocks
    for b in range(0, tile, rows):
        row = at + b
        move.block(pos[piece, row // rows], blocks, stage.at[pl.ds(row, rows), :], keep, send)


def grad_into(move, pos, lefts, rights, stages, outs):
    width = stages[0].shape[0]
    tile = 256
    for at in range(0, width, tile):
        for piece in range(2):
            col = 0
            for left, right in zip(lefts[piece], rights[piece]):
                value = tn(left[:, at : at + tile], right).astype(BF)
                stages[piece][at : at + tile, col : col + right.shape[1]] = value
                col += right.shape[1]
            grad_tiles(move, pos, tile, at, 0, stages[piece], outs[2 * piece], outs[2 * piece + 1], piece)


def mlp_up_kernel(
    ids, pos, own_hbm, other_hbm, r_hbm, vec_hbm, gate_hbm, g_hbm, s0, s1, s2, s3,
    h_hbm, n2_hbm, slope_hbm, z_hbm, dm_hbm, k0, d0, k1, d1,
    own, other, r, vec, gate, g, h, n2, slope, z, dm, weights, stage0, stage1, sem,
):
    move = Mover(sem)
    early = move.fetch([(own_hbm, own), (other_hbm, other), (r_hbm, r), (vec_hbm, vec)])
    copies = move.weights(ids, (s0, s1, s2, s3), weights)
    late = move.fetch([(gate_hbm, gate), (g_hbm, g)])
    wait(early)
    h[...] = r[...].astype(F32) + (own[...].astype(F32) + other[...].astype(F32))
    move.put(h, h_hbm)
    normal = h[...] * lax.rsqrt(jnp.mean(h[...] * h[...], axis=-1, keepdims=True) + epsilon)
    n2[...] = (normal * vec[1:2]).astype(BF)
    move.put(n2, n2_hbm)
    wait(copies)
    wait(late)
    dm[...] = (gate[:, :1] * g[...].astype(F32)).astype(BF)
    move.put(dm, dm_hbm)
    a, c = 0.044715, 0.7978845608028654
    step = 512
    for at in range(0, weights.shape[1], step):
        cols = slice(at, at + step)
        u = nn(n2[...], weights[:, cols])
        square = u * u
        t = jnp.tanh(c * (u + a * (square * u)))
        half = 0.5 * (1.0 + t)
        z[:, cols] = (u * half).astype(BF)
        slope[:, cols] = half + 0.5 * u * (1.0 - t * t) * (c * (1.0 + 3.0 * a * square))
        move.put(slope.at[:, pl.ds(at, step)], slope_hbm.at[:, pl.ds(at, step)])
    move.put(z, z_hbm)
    cut = stage0.shape[1]
    grad_into(move, pos, [[dm], [dm]], [[z[:, :cut]], [z[:, cut:]]], (stage0, stage1), (k0, d0, k1, d1))
    move.finish()


def places_of(width, n):
    if (width // n) % 16 == 0:
        return jnp.stack([places(n, o) for o in color_orders(n)])
    return jnp.zeros((2, 16), jnp.int32) + jnp.arange(16, dtype=jnp.int32)


def grad_shapes(width, total):
    cut = split_of(total)
    outs = [((width // 2, c), BF) for c in (cut, cut, total - cut, total - cut)]
    return outs, [like((width, cut)), like((width, total - cut))]


def scatter_of(outs, width, n):
    keep0, send0, keep1, send1 = outs
    keep, send = [keep0, keep1], [send0, send1]
    if (width // n) % 16:
        orders = color_orders(n)
        for at in range(2):
            whole = jnp.concatenate([keep[at], send[at]], axis=0).reshape(n, width // n, -1)
            whole = whole[owners(n, orders[at])].reshape(width, -1)
            keep[at], send[at] = whole[: width // 2], whole[width // 2 :]
    return Scatter(keep, send, n)


def mlp_up(source, pos, own, other, routed, upstream, gate, vec, hidden, n):
    ids, halves = source
    rows, width = routed.shape
    outs = [((rows, width), F32), ((rows, width), BF), ((rows, hidden), F32), ((rows, hidden), BF), ((rows, width), BF)]
    grad, stages = grad_shapes(width, hidden)
    result = hbm_call(
        mlp_up_kernel,
        [sds(*o) for o in outs + grad],
        (ids, pos),
        (own, other, routed, vec, gate, upstream, *halves),
        [like((rows, width))] * 3
        + [like((8, width), F32), like((rows, LANE), F32), like((rows, width))]
        + [like(*o) for o in outs]
        + [like((width, hidden))]
        + stages,
        2 * ids.shape[1] + 2 * pos.shape[1] + 16,
        "mlp_up",
        44,
    )
    return result[:5], scatter_of(result[5:], width, n)


def mlp_back_kernel(
    idu, idd, dm_hbm, slope_hbm, u0, u1, u2, u3, d0, d1, d2, d3, du_hbm, part_hbm, dm, slope, du, part, wu, wd, sem
):
    move = Mover(sem)
    step = 512
    first = move.fetch([(dm_hbm, dm)])
    down = move.weights(idd, (d0, d1, d2, d3), wd)
    tiles = [
        move.fetch([(slope_hbm.at[:, pl.ds(at, step)], slope.at[:, pl.ds(at, step)])])
        for at in range(0, wd.shape[1], step)
    ]
    up = move.weights(idu, (u0, u1, u2, u3), wu)
    wait(first)
    wait(down)
    for at in range(0, wd.shape[1], step):
        dz = nn(dm[...], wd[:, at : at + step])
        wait(tiles[at // step])
        du[:, at : at + step] = (dz * slope[:, at : at + step]).astype(BF)
    move.put(du, du_hbm)
    wait(up)
    half = part.shape[0] // 2
    for at in range(0, part.shape[0], half):
        part[at : at + half] = nt(du[at : at + half], wu[...]).astype(BF)
        move.put(part.at[pl.ds(at, half)], part_hbm.at[pl.ds(at, half)])
    move.finish()


def mlp_back(up, down, dm, slope):
    rows, width = dm.shape
    hidden = slope.shape[1]
    return hbm_call(
        mlp_back_kernel,
        [sds((rows, hidden), BF), sds((rows, width), BF)],
        (up[0], down[0]),
        (dm, slope, *up[1], *down[1]),
        [like((rows, width)), like((rows, hidden), F32), like((rows, hidden)), like((rows, width))]
        + [like((width, hidden))] * 2,
        4 * up[0].shape[1] + 16,
        "mlp_back",
        36,
    )


def grad_up_kernel(pos, n2_hbm, du_hbm, k0, d0, k1, d1, n2, du, stage0, stage1, sem):
    move = Mover(sem)
    wait(move.fetch([(n2_hbm, n2), (du_hbm, du)]))
    cut = stage0.shape[1]
    grad_into(move, pos, [[n2], [n2]], [[du[:, :cut]], [du[:, cut:]]], (stage0, stage1), (k0, d0, k1, d1))
    move.finish()


def grad_up(pos, n2, du, n):
    rows, width = n2.shape
    hidden = du.shape[1]
    grad, stages = grad_shapes(width, hidden)
    result = hbm_call(
        grad_up_kernel,
        [sds(*o) for o in grad],
        (pos,),
        (n2, du),
        [like((rows, width)), like((rows, hidden))] + stages,
        2 * pos.shape[1] + 4,
        "grad_up",
        24,
    )
    return scatter_of(result, width, n)


def mlp_out_kernel(idd, z_hbm, d0, d1, d2, d3, part_hbm, z, wd, part, sem):
    move = Mover(sem)
    first = move.fetch([(z_hbm, z)])
    wait(move.weights(idd, (d0, d1, d2, d3), wd))
    wait(first)
    half = part.shape[0] // 2
    for at in range(0, part.shape[0], half):
        part[at : at + half] = nt(z[at : at + half], wd[...]).astype(BF)
        move.put(part.at[pl.ds(at, half)], part_hbm.at[pl.ds(at, half)])
    move.finish()


def mlp_out(down, z, width):
    rows, hidden = z.shape
    return hbm_call(
        mlp_out_kernel,
        [sds((rows, width), BF)],
        (down[0],),
        (z, *down[1]),
        [like((rows, hidden)), like((width, hidden)), like((rows, width))],
        2 * down[0].shape[1] + 8,
        "mlp_out",
        24,
    )[0]


def attn_back_kernel(
    ids, pos, own_hbm, other_hbm, h_hbm, vec_hbm, gate_hbm, g_hbm, qkv_hbm, p_hbm, n1_hbm, o_hbm, s0, s1, s2, s3,
    dh_hbm, part_hbm, gain_hbm, k0, d0, k1, d1,
    own, other, h, vec, gate, g, qkv, prob, n1, o, dh, part, gain_out, weights, da, do_ref, dqkv, stage0, stage1, sem,
):
    move = Mover(sem)
    early = move.fetch([(h_hbm, h), (own_hbm, own), (other_hbm, other), (vec_hbm, vec), (gate_hbm, gate), (g_hbm, g)])
    copies = move.weights(ids, (s0, s1, s2, s3), weights)
    heads_in = move.fetch([(qkv_hbm, qkv), (p_hbm, prob)])
    late = move.fetch([(o_hbm, o), (n1_hbm, n1)])
    rows = h.shape[0]
    w = do_ref.shape[1]
    wait(early)
    dn2 = own[...].astype(F32) + other[...].astype(F32)
    inverse = lax.rsqrt(jnp.mean(h[...] * h[...], axis=-1, keepdims=True) + epsilon)
    normal = h[...] * inverse
    product = dn2 * normal
    gain_out[...] = jnp.broadcast_to(jnp.sum(product, axis=0, keepdims=True), gain_out.shape)
    move.put(gain_out, gain_hbm)
    gain = vec[1:2]
    dh[...] = inverse * (dn2 * gain - normal * jnp.mean(product * gain, axis=-1, keepdims=True))
    move.put(dh, dh_hbm)
    da[...] = (gate[:, :1] * g[...].astype(F32) + dh[...]).astype(BF)
    wait(copies)
    do_ref[...] = nn(da[...], weights[:, 3 * w : 4 * w]).astype(BF)
    wait(heads_in)
    first = lax.broadcasted_iota(jnp.int32, (CAP, 2 * HD), 1) < HD
    scale = HD**-0.5
    pairs = w // (2 * HD)
    for s in range(rows // CAP):
        at_rows = slice(s * CAP, (s + 1) * CAP)
        for pair in range(pairs):
            at = pair * 2 * HD
            q = qkv[at_rows, at : at + 2 * HD]
            k = qkv[at_rows, w + at : w + at + 2 * HD]
            v = qkv[at_rows, 2 * w + at : 2 * w + at + 2 * HD]
            do = do_ref[at_rows, at : at + 2 * HD]
            zero = jnp.zeros_like(q)
            results = []
            for head in range(2):
                do_one = jnp.where(first, do, zero) if head == 0 else jnp.where(first, zero, do)
                probability = prob[2 * (s * pairs + pair) + head]
                d_probability = nt(do_one, v)
                dv = tn(probability.astype(BF), do)
                inner = jnp.sum(probability * d_probability, axis=-1, keepdims=True)
                ds = (probability * (d_probability - inner)).astype(BF)
                results.append((nn(ds, k) * scale, tn(ds, q) * scale, dv))
            for which in range(3):
                value = jnp.where(first, results[0][which], results[1][which]).astype(BF)
                dqkv[at_rows, which * w + at : which * w + at + 2 * HD] = value
    wait(late)
    cut = stage0.shape[1]
    grad_into(
        move, pos, [[n1], [n1, da]], [[dqkv[:, :cut]], [dqkv[:, cut:], o[...]]], (stage0, stage1), (k0, d0, k1, d1)
    )
    part[...] = nt(dqkv[...], weights[:, : 3 * w]).astype(BF)
    move.put(part, part_hbm)
    move.finish()


def attn_back(source, pos, own, other, h, vec, upstream, gate, qkv, prob, n1, attended, n):
    ids, halves = source
    rows, width = h.shape
    w = attended.shape[1]
    grad, stages = grad_shapes(width, 4 * w)
    ins = (own, other, h, vec, gate, upstream, qkv, prob, n1, attended)
    outs = [((rows, width), F32), ((rows, width), BF), ((8, width), F32)]
    result = hbm_call(
        attn_back_kernel,
        [sds(*o) for o in outs + grad],
        (ids, pos),
        (*ins, *halves),
        [like(x.shape, x.dtype) for x in ins]
        + [like(*o) for o in outs]
        + [like((width, 4 * w + EXTRA)), like((rows, width)), like((rows, w)), like((rows, 3 * w))]
        + stages,
        2 * ids.shape[1] + 2 * pos.shape[1] + 16,
        "attn_back",
        48,
    )
    return result[:3], scatter_of(result[3:], width, n)


TILE = 512


def select_rows(slot_ref, sel, rows, x_ref, out_ref):
    place = lax.broadcasted_iota(jnp.int32, (CAP, LANE), 0).astype(F32)
    for at in range(TILE // LANE):
        sel[:, at * LANE : (at + 1) * LANE] = jnp.where(place == slot_ref[at], 1.0, 0.0).astype(BF)
    put = tn(sel[...], rows[...])
    hit = tn(sel[...], jnp.ones((CAP, LANE), BF))[:, :1]
    out_ref[...] = jnp.where(hit > 0.5, put.astype(BF), x_ref[...])


def rows_out_kernel(
    count_ref, slot_ref, x_ref, attn_own, attn_other, own, other, r_ref, g_ref, gate_ref,
    out_ref, dl_ref, router_ref, sum_ref, rows, sel,
):
    s, t = pl.program_id(0), pl.program_id(1)

    @pl.when(t == 0)
    def _():
        inputs = r_ref[...].astype(F32)
        gate = gate_ref[:, :1]
        attention = attn_own[...].astype(F32) + attn_other[...].astype(F32)
        branch = attention + (own[...].astype(F32) + other[...].astype(F32))
        rows[...] = (inputs + gate * branch).astype(BF)
        dl = jnp.sum(g_ref[...].astype(F32) * branch, axis=-1, keepdims=True) * gate * (1.0 - gate)
        dl_ref[...] = jnp.broadcast_to(dl, dl_ref.shape)
        router_ref[0] = jnp.broadcast_to(jnp.sum(dl * inputs, axis=0, keepdims=True), router_ref.shape[1:])
        row = lax.broadcasted_iota(jnp.int32, (CAP, LANE), 0)
        total = jnp.sum(jnp.where(row < count_ref[s], gate_ref[...], 0.0), axis=0, keepdims=True)
        sum_ref[0] = jnp.broadcast_to(total, sum_ref.shape[1:])

    select_rows(slot_ref, sel, rows, x_ref, out_ref)


def rows_back_kernel(slot_ref, x_ref, own, other, r_ref, g_ref, dl_ref, dh_ref, vec_ref, out_ref, gain_ref, rows, sel):
    @pl.when(pl.program_id(1) == 0)
    def _():
        inputs = r_ref[...].astype(F32)
        dn1 = own[...].astype(F32) + other[...].astype(F32)
        inverse = lax.rsqrt(jnp.mean(inputs * inputs, axis=-1, keepdims=True) + epsilon)
        normal = inputs * inverse
        product = dn1 * normal
        gain_ref[0] = jnp.broadcast_to(jnp.sum(product, axis=0, keepdims=True), gain_ref.shape[1:])
        gain = vec_ref[0:1]
        dr = inverse * (dn1 * gain - normal * jnp.mean(product * gain, axis=-1, keepdims=True))
        total = g_ref[...].astype(F32) + dh_ref[...] + dl_ref[:, :1] * vec_ref[2:3] + dr
        rows[...] = total.astype(BF)

    select_rows(slot_ref, sel, rows, x_ref, out_ref)


def tiled(kernel, counts, slot, tokens, by_row, whole, outs, name):
    width = tokens.shape[1]
    per = LEN // TILE
    seqs = tokens.shape[0] // LEN
    groups = TILE // LANE
    row_spec = lambda shape: pl.BlockSpec((CAP, shape[1]), lambda s, t: (s, 0))
    one_spec = lambda shape: pl.BlockSpec((1,) + shape[1:], lambda s, t: (s, 0, 0))
    return pl.pallas_call(
        kernel,
        grid=(seqs, per),
        in_specs=[SM] * len(counts)
        + [
            pl.BlockSpec((groups, 1, LANE), lambda s, t: (s * per + t, 0, 0)),
            pl.BlockSpec((TILE, width), lambda s, t: (s * per + t, 0)),
        ]
        + [row_spec(a.shape) for a in by_row]
        + [pl.BlockSpec(a.shape, lambda s, t: (0, 0)) for a in whole],
        out_specs=[pl.BlockSpec((TILE, width), lambda s, t: (s * per + t, 0))]
        + [row_spec(o.shape) if len(o.shape) == 2 else one_spec(o.shape) for o in outs],
        out_shape=[sds(tokens.shape, BF)] + outs,
        scratch_shapes=[pltpu.VMEM((CAP, width), BF), pltpu.VMEM((CAP, TILE), BF)],
        compiler_params=pltpu.CompilerParams(vmem_limit_bytes=56 * MIB),
        cost_estimate=COST,
        name=name,
    )(*counts, slot, tokens, *by_row, *whole)


def rows_out(counts, slot, tokens, attn_own, attn_other, own, other, routed, upstream, gate):
    seqs, width = counts.shape[0], routed.shape[1]
    outs = [sds((routed.shape[0], LANE), F32), sds((seqs, 8, width), F32), sds((seqs, 8, LANE), F32)]
    by_row = (attn_own, attn_other, own, other, routed, upstream, gate)
    return tiled(rows_out_kernel, (counts,), slot, tokens, by_row, (), outs, "rows_out")


def rows_back(slot, tokens, own, other, routed, upstream, dl, dh, vec):
    outs = [sds((tokens.shape[0] // LEN, 8, routed.shape[1]), F32)]
    by_row = (own, other, routed, upstream, dl, dh)
    return tiled(rows_back_kernel, (), slot, tokens, by_row, (vec,), outs, "rows_back")


def body(
    tokens_in,
    route_mask,
    cotangent,
    w_query,
    w_key,
    w_value,
    w_out,
    w_up,
    w_down,
    gain_attn,
    gain_mlp,
    router,
):
    n = lax.axis_size("dp")
    mine, w = w_query.shape
    hidden = w_up.shape[1]
    width = tokens_in.shape[1]
    seqs = tokens_in.shape[0] // LEN
    extras = jnp.concatenate(
        [gain_attn[:, None], gain_mlp[:, None], router[:, None], jnp.zeros((mine, EXTRA - 3), BF)], axis=1
    )
    attn = Gather(jnp.concatenate([w_query, w_key, w_value, w_out.T, extras], axis=1), n)
    up = Gather(w_up, n)
    down = Gather(w_down.T, n)
    counts = jnp.sum(route_mask.reshape(seqs, LEN), axis=1).astype(jnp.int32)

    def start(chains, token, swaps=()):
        held = [c.held if isinstance(c, Gather) else c.send for c in chains]
        flat = tie([v for h in held for v in h] + list(swaps), token)
        arrived = []
        for chain, h in zip(chains, held):
            part, flat = flat[: len(h)], flat[len(h) :]
            if isinstance(chain, Gather):
                chain.held = part
            else:
                chain.send = part
            arrived += chain.begin()
        swapped = [other_core(v) for v in flat]
        return arrived + swapped, swapped

    def close(chains, made=()):
        flat = tie([g for c in chains for g in c.got], made)
        for chain in chains:
            chain.got, flat = flat[: len(chain.got)], flat[len(chain.got) :]
            chain.end()

    pos = places_of(width, n)
    four = attn.steps == 4

    token, _ = start([attn], [])
    routed, upstream, slot = pick(route_mask, tokens_in, cotangent, seqs)
    close([attn], [slot])
    for chains in ([attn, up], [attn, up], [attn, down]) if four else [[attn, up, down]] * (attn.steps - 1):
        token, _ = start(chains, token)
        close(chains)
    src_attn = attn.result()
    rest = [[up, down], [up, down], [down]] if four else [[up, down], [], []]
    token, _ = start(rest[0], token)
    n1, qkv, attended, attn_own, gate, vec, prob = attn_fwd(src_attn, counts, routed, w)
    close(rest[0], [attn_own])
    token, (attn_other,) = start(rest[1], token, [attn_own])
    close(rest[1])
    src_up = up.result()
    token, _ = start(rest[2], token)
    (h, n2, slope, z, dm), sum_down = mlp_up(
        src_up, pos, attn_own, attn_other, routed, upstream, gate, vec, hidden, n
    )
    close(rest[2], [dm])
    src_down = down.result()

    token, _ = start([sum_down], token)
    du, dn2_own = mlp_back(src_up, src_down, dm, slope)
    close([sum_down], [du])
    token, (dn2_other,) = start([sum_down], token, [dn2_own])
    sum_up = grad_up(pos, n2, du, n)
    close([sum_down], sum_up.send)
    token, _ = start([sum_up, sum_down], token)
    (dh, dn1_own, gain_two), sum_attn = attn_back(
        src_attn, pos, dn2_own, dn2_other, h, vec, upstream, gate, qkv, prob, n1, attended, n
    )
    close([sum_up, sum_down], [dh])
    token, (dn1_other,) = start([sum_attn, sum_up, sum_down], token, [dn1_own])
    (z_late,) = tie([z], [dn1_other])
    feed_own = mlp_out(src_down, z_late, width)
    close([sum_attn, sum_up, sum_down], [feed_own])
    live = [c for c in (sum_attn, sum_up, sum_down) if c.at]
    token, (feed_other,) = start(live, token, [feed_own])
    block_out, dl, d_router, gate_sum = rows_out(
        counts, slot, tokens_in, attn_own, attn_other, feed_own, feed_other, routed, upstream, gate
    )
    close(live, [dl])
    live = [c for c in live if c.at]
    token, _ = start(live, token + [dl])
    (dl_late,) = tie([dl], [token[0]])
    input_grad, gain_one = rows_back(slot, cotangent, dn1_own, dn1_other, routed, upstream, dl_late, dh, vec)
    scalars = jnp.stack([jnp.sum(counts).astype(F32), jnp.sum(gate_sum[:, 0, 0])])
    small = jnp.concatenate(
        [
            jnp.sum(gain_one[:, 0], axis=0).reshape(n, mine),
            gain_two[0].reshape(n, mine),
            jnp.sum(d_router[:, 0], axis=0).reshape(n, mine),
            jnp.broadcast_to(scalars, (n, 2)),
        ],
        axis=1,
    )
    small = jnp.sum(lax.all_to_all(small, "dp", 0, 0, tiled=True), axis=0)
    close(live, [gain_one])
    live = [c for c in live if c.at]
    token = token + [gain_one]
    while live:
        token, _ = start(live, token)
        close(live)
        live = [c for c in live if c.at]
    total_attn, total_up, total_down = sum_attn.result(), sum_up.result(), sum_down.result()
    token_total = tokens_in.shape[0] * n
    return (
        block_out,
        input_grad,
        total_attn[:, :w],
        total_attn[:, w : 2 * w],
        total_attn[:, 2 * w : 3 * w],
        total_attn[:, 3 * w :].T,
        total_up,
        total_down.T,
        small[:mine],
        small[mine : 2 * mine],
        small[2 * mine : 3 * mine],
        small[3 * mine] / token_total,
        small[3 * mine + 1] / small[3 * mine],
    )


def solution(mesh):
    rows, cols = P("dp", "mp"), P("mp", "dp")
    return jax.shard_map(
        body,
        mesh=mesh,
        in_specs=(P("dp", None), P("dp"), P("dp", None), rows, rows, rows, cols, rows, cols) + (P("dp"),) * 3,
        out_specs=(P("dp", None), P("dp", None), rows, rows, rows, cols, rows, cols) + (P("dp"),) * 3 + (P(), P()),
        check_vma=False,
    )
```

```python
import jax
import jax.numpy as jnp
from jax import lax
from jax.experimental import pallas as pl
from jax.experimental.pallas import tpu as pltpu
from jax.sharding import PartitionSpec as P

HD = 64
LEN = 2048
CAP = 256
LANE = 128
EXTRA = 128
MIB = 1 << 20
LIMITS = (20, 28, 24, 12, 14, 34, 24, 46, 24)
COST = pl.CostEstimate(flops=8000000000, bytes_accessed=24000000, transcendentals=0)

epsilon = 1e-06
negative = -1e30
BF = jnp.bfloat16
F32 = jnp.float32
SM = pl.BlockSpec(memory_space=pltpu.SMEM)
HB = pl.BlockSpec(memory_space=pltpu.HBM)
VM = pl.BlockSpec(memory_space=pltpu.VMEM)
ANY = pl.BlockSpec(memory_space=pl.ANY)


def nn(a, b):
    return jnp.dot(a, b, preferred_element_type=F32)


def nt(a, b):
    return lax.dot_general(a, b, (((1,), (1,)), ((), ())), preferred_element_type=F32)


def tn(a, b):
    return lax.dot_general(a, b, (((0,), (0,)), ((), ())), preferred_element_type=F32)


def sds(shape, dtype):
    return jax.ShapeDtypeStruct(shape, dtype)


def color_orders(n):
    bits = n.bit_length() - 1
    if bits == 4:
        x, y, z1, z2 = 1, 2, 4, 8
        return (((z2, y, z1, x), (z2, z1, x, y)), ((z2, x, y, z1), (z2, x, y, z1)))
    down = tuple(1 << b for b in reversed(range(bits)))
    return ((down, down), (down, down))


def bit_sum(n, index, source, target):
    total = jnp.zeros((n,), jnp.int32)
    for one, two in zip(source, target):
        total = total | jnp.where((index & one) != 0, two, 0)
    return total


def spots(orders):
    return [1 << k for k in range(len(orders[0]))]


def owners(n, orders):
    p = jnp.arange(n, dtype=jnp.int32)
    one, two = (bit_sum(n, p, spots(orders), o) for o in orders)
    return lax.axis_index("dp") ^ jnp.where(lax.axis_index("mp") == 0, one, two)


def places(n, orders):
    d = jnp.arange(n, dtype=jnp.int32) ^ lax.axis_index("dp")
    one, two = (bit_sum(n, d, o, spots(orders)) for o in orders)
    return jnp.where(lax.axis_index("mp") == 0, one, two)


def hop(array, n, one, two):
    pairs = [(d * 2 + c, (d ^ (one, two)[c]) * 2 + c) for d in range(n) for c in range(2)]
    return lax.ppermute(array, ("dp", "mp"), pairs)


def other_core(array):
    return lax.ppermute(array, "mp", [(0, 1), (1, 0)])


def split_of(width):
    return -(-width * 2 // (3 * LANE)) * LANE


class Gather:
    def __init__(self, shard, n):
        self.n = n
        self.orders = color_orders(n)
        self.steps = len(self.orders[0][0])
        self.at = 0
        self.width = shard.shape[1]
        self.cut = split_of(self.width)
        self.held = [shard]
        self.got = None

    def begin(self):
        k = self.at
        if k == 0:
            one, two = self.orders[0][0][0], self.orders[0][1][0]
            self.got = [hop(self.held[0], self.n, one, two)]
        else:
            self.got = [hop(h, self.n, o[0][k], o[1][k]) for h, o in zip(self.held, self.orders)]
        self.at += 1
        return self.got

    def end(self):
        if self.at == self.steps:
            return
        if self.at == 1:
            both = jnp.concatenate([self.held[0], self.got[0]], axis=0)
            self.held = [both[:, : self.cut], both[:, self.cut :]]
        else:
            self.held = [jnp.concatenate([h, g], axis=0) for h, g in zip(self.held, self.got)]

    def result(self):
        n = self.n
        ids = jnp.stack([owners(n, o) for o in self.orders])
        halves = [self.held[0], self.got[0], self.held[1], self.got[1]]
        rows = 2 * self.held[0].shape[0]
        if (rows // n) % 16:
            out = []
            for at, (h, g) in enumerate(zip(self.held, self.got)):
                blocks = jnp.concatenate([h, g], axis=0).reshape(n, rows // n, -1)
                blocks = blocks[places(n, self.orders[at])].reshape(rows, -1)
                out += [blocks[: rows // 2], blocks[rows // 2 :]]
            return jnp.zeros((2, 2), jnp.int32) + jnp.arange(2, dtype=jnp.int32), out
        return ids, halves


class Scatter:
    def __init__(self, keep, send, n):
        self.n = n
        self.orders = color_orders(n)
        self.steps = len(self.orders[0][0])
        self.at = self.steps
        self.keep, self.send = keep, send

    def ops(self):
        return self.send

    def begin(self):
        k = self.at - 1
        if len(self.send) == 1:
            one, two = self.orders[0][0][0], self.orders[0][1][0]
            self.got = [hop(self.send[0], self.n, one, two)]
        else:
            self.got = [hop(s, self.n, o[0][k], o[1][k]) for s, o in zip(self.send, self.orders)]
        self.at -= 1
        return self.got

    def end(self):
        half = self.got[0].shape[0] // 2
        if self.at == 0:
            self.keep = [k.astype(F32) + g.astype(F32) for k, g in zip(self.keep, self.got)]
            self.send = []
            return
        send = [(k[half:].astype(F32) + g[half:].astype(F32)).astype(BF) for k, g in zip(self.keep, self.got)]
        keep = [(k[:half].astype(F32) + g[:half].astype(F32)).astype(BF) for k, g in zip(self.keep, self.got)]
        if self.at == 1:
            keep = [jnp.concatenate(keep, axis=1)]
            send = [jnp.concatenate(send, axis=1)]
        self.keep, self.send = keep, send

    def result(self):
        return self.keep[0]


def tie(values, tokens):
    if not tokens:
        return list(values)
    out = lax.optimization_barrier(tuple(values) + tuple(tokens))
    return list(out[: len(values)])


def pick_kernel(mask_ref, x_ref, c_ref, r_ref, g_ref, slot_ref, sel):
    groups = mask_ref.shape[1]
    flag = mask_ref[0].astype(F32)
    up = lax.broadcasted_iota(jnp.int32, (LANE, LANE), 0) <= lax.broadcasted_iota(jnp.int32, (LANE, LANE), 1)
    within = nn(flag, up.astype(F32))
    total = jnp.broadcast_to(within[:, LANE - 1 :], (groups, LANE))
    low = lax.broadcasted_iota(jnp.int32, (groups, groups), 1) < lax.broadcasted_iota(
        jnp.int32, (groups, groups), 0
    )
    rank = within + nn(low.astype(F32), total) - 1.0
    slot = jnp.where(flag > 0, rank, -1.0)
    place = lax.broadcasted_iota(jnp.int32, (CAP, LANE), 0).astype(F32)
    for at in range(groups):
        slot_ref[at] = slot[at : at + 1]
        sel[:, at * LANE : (at + 1) * LANE] = jnp.where(place == slot[at : at + 1], 1.0, 0.0).astype(BF)
    r_ref[...] = nn(sel[...], x_ref[...]).astype(BF)
    g_ref[...] = nn(sel[...], c_ref[...]).astype(BF)


def pick(mask, tokens, cotangent, seqs):
    width = tokens.shape[1]
    groups = LEN // LANE
    return pl.pallas_call(
        pick_kernel,
        grid=(seqs,),
        in_specs=[
            pl.BlockSpec((1, groups, LANE), lambda s: (s, 0, 0)),
            pl.BlockSpec((LEN, width), lambda s: (s, 0)),
            pl.BlockSpec((LEN, width), lambda s: (s, 0)),
        ],
        out_specs=[
            pl.BlockSpec((CAP, width), lambda s: (s, 0)),
            pl.BlockSpec((CAP, width), lambda s: (s, 0)),
            pl.BlockSpec((groups, 1, LANE), lambda s: (s, 0, 0)),
        ],
        out_shape=[
            sds((seqs * CAP, width), BF),
            sds((seqs * CAP, width), BF),
            sds((seqs * groups, 1, LANE), F32),
        ],
        scratch_shapes=[pltpu.VMEM((CAP, LEN), BF)],
        compiler_params=pltpu.CompilerParams(vmem_limit_bytes=LIMITS[7] * MIB),
        cost_estimate=COST,
        name="pick",
    )(mask.reshape(seqs, groups, LANE), tokens, cotangent)


class Mover:
    def __init__(self, sem):
        self.sem = sem
        self.used = 0
        self.out = []

    def start(self, src, dst):
        copy = pltpu.make_async_copy(src, dst, self.sem.at[self.used])
        self.used += 1
        copy.start()
        return copy

    def put(self, src, dst):
        self.out.append(self.start(src, dst))

    def weights(self, ids_ref, halves, dst):
        blocks = ids_ref.shape[1]
        rows = dst.shape[0] // blocks
        copies = []
        col = 0
        for piece in range(2):
            width = halves[2 * piece].shape[1]
            for at in range(blocks):
                src = halves[2 * piece + at // (blocks // 2)]
                from_row = (at % (blocks // 2)) * rows
                to_row = pl.multiple_of(ids_ref[piece, at] * rows, rows)
                copies.append(
                    self.start(src.at[pl.ds(from_row, rows), :], dst.at[pl.ds(to_row, rows), pl.ds(col, width)])
                )
            col += width
        return copies

    def finish(self):
        wait(self.out)


def wait(copies):
    for copy in copies:
        copy.wait()


def like(shape, dtype=BF):
    return pltpu.VMEM(shape, dtype)


def call(kernel, out_shape, out_specs, args, in_specs, scratch, copies, name, limit):
    return pl.pallas_call(
        kernel,
        out_shape=out_shape,
        in_specs=in_specs,
        out_specs=out_specs,
        scratch_shapes=list(scratch) + [pltpu.SemaphoreType.DMA((copies,))],
        compiler_params=pltpu.CompilerParams(vmem_limit_bytes=limit * MIB),
        cost_estimate=COST,
        name=name,
    )(*args)


def softmax(queries, keys, allowed):
    scores = nt(queries, keys) * (HD**-0.5)
    scores = jnp.where(allowed, scores, negative)
    raised = jnp.exp(scores - jnp.max(scores, axis=-1, keepdims=True))
    return raised / jnp.sum(raised, axis=-1, keepdims=True)


def allowed_slots(count):
    row = lax.broadcasted_iota(jnp.int32, (CAP, CAP), 0)
    col = lax.broadcasted_iota(jnp.int32, (CAP, CAP), 1)
    return (col <= row) & (col < count)


def attn_fwd_kernel(
    ids, count_ref, r, s0, s1, s2, s3, n1, qkv, o, part, gate, vec, p_hbm, weights, prob, sem
):
    move = Mover(sem)
    copies = move.weights(ids, (s0, s1, s2, s3), weights)
    w = o.shape[1]
    seqs = r.shape[0] // CAP
    inputs = r[...].astype(F32)
    normal = inputs * lax.rsqrt(jnp.mean(inputs * inputs, axis=-1, keepdims=True) + epsilon)
    wait(copies)
    vectors = weights[:, 4 * w :].astype(F32).T[:8]
    vec[...] = vectors
    n1[...] = (normal * vectors[0:1]).astype(BF)
    logit = jnp.sum(inputs * vectors[2:3], axis=-1, keepdims=True)
    gate[...] = jnp.broadcast_to(jax.nn.sigmoid(logit), gate.shape)
    qkv[...] = nn(n1[...], weights[:, : 3 * w]).astype(BF)
    first = lax.broadcasted_iota(jnp.int32, (CAP, 2 * HD), 1) < HD
    pairs = w // (2 * HD)
    for s in range(seqs):
        allowed = allowed_slots(count_ref[s])
        rows = slice(s * CAP, (s + 1) * CAP)
        for pair in range(pairs):
            at = pair * 2 * HD
            q = qkv[rows, at : at + 2 * HD]
            k = qkv[rows, w + at : w + at + 2 * HD]
            v = qkv[rows, 2 * w + at : 2 * w + at + 2 * HD]
            zero = jnp.zeros_like(q)
            one = softmax(jnp.where(first, q, zero), k, allowed)
            two = softmax(jnp.where(first, zero, q), k, allowed)
            head = 2 * (s * pairs + pair)
            prob[head] = one
            prob[head + 1] = two
            o[rows, at : at + 2 * HD] = jnp.where(first, nn(one.astype(BF), v), nn(two.astype(BF), v)).astype(BF)
        half = pl.ds(2 * s * pairs, 2 * pairs)
        move.put(prob.at[half], p_hbm.at[half])
    part[...] = nt(o[...], weights[:, 3 * w : 4 * w]).astype(BF)
    move.finish()


def attn_fwd(source, counts, routed, w):
    ids, halves = source
    rows, width = routed.shape
    heads = rows // CAP * w // HD
    outs = [
        sds((rows, width), BF), sds((rows, 3 * w), BF), sds((rows, w), BF), sds((rows, width), BF),
        sds((rows, LANE), F32), sds((8, width), F32), sds((heads, CAP, CAP), F32),
    ]
    return call(
        attn_fwd_kernel, outs, [VM] * 6 + [HB],
        (ids, counts, routed, *halves), [SM, SM, VM] + [ANY] * 4,
        [like((width, 4 * w + EXTRA)), like((heads, CAP, CAP), F32)],
        2 * ids.shape[1] + 4, "attn_fwd", LIMITS[0],
    )


def grad_into(pos, lefts, rights, outs):
    blocks = pos.shape[1]
    width = 2 * outs[0].shape[0]
    rows = width // blocks
    tile = 256
    for at in range(0, width, tile):
        for piece in range(2):
            keep, send = outs[2 * piece], outs[2 * piece + 1]
            col = 0
            for left, right in zip(lefts[piece], rights[piece]):
                value = tn(left[:, at : at + tile], right).astype(BF)
                cols = slice(col, col + right.shape[1])
                col += right.shape[1]
                for b in range(0, tile, rows):
                    place = pos[piece, (at + b) // rows]
                    block = value[b : b + rows]

                    @pl.when(place < blocks // 2)
                    def _():
                        keep[pl.ds(pl.multiple_of(place * rows, rows), rows), cols] = block

                    @pl.when(place >= blocks // 2)
                    def _():
                        send[pl.ds(pl.multiple_of((place - blocks // 2) * rows, rows), rows), cols] = block


def mlp_up_kernel(
    ids, pos, own, other, r, vec, gate, g, s0, s1, s2, s3,
    h_hbm, n2, slope_hbm, z_hbm, dm, k0, d0, k1, d1, h, slope, z, weights, sem,
):
    move = Mover(sem)
    copies = move.weights(ids, (s0, s1, s2, s3), weights)
    h[...] = r[...].astype(F32) + (own[...].astype(F32) + other[...].astype(F32))
    move.put(h, h_hbm)
    normal = h[...] * lax.rsqrt(jnp.mean(h[...] * h[...], axis=-1, keepdims=True) + epsilon)
    n2[...] = (normal * vec[1:2]).astype(BF)
    dm[...] = (gate[:, :1] * g[...].astype(F32)).astype(BF)
    wait(copies)
    a, c = 0.044715, 0.7978845608028654
    step = 512
    for at in range(0, weights.shape[1], step):
        cols = slice(at, at + step)
        u = nn(n2[...], weights[:, cols])
        square = u * u
        t = jnp.tanh(c * (u + a * (square * u)))
        half = 0.5 * (1.0 + t)
        z[:, cols] = (u * half).astype(BF)
        slope[:, cols] = half + 0.5 * u * (1.0 - t * t) * (c * (1.0 + 3.0 * a * square))
        move.put(slope.at[:, pl.ds(at, step)], slope_hbm.at[:, pl.ds(at, step)])
    move.put(z, z_hbm)
    cut = k0.shape[1]
    grad_into(pos, [[dm], [dm]], [[z[:, :cut]], [z[:, cut:]]], (k0, d0, k1, d1))
    move.finish()


def places_of(width, n):
    if (width // n) % 16 == 0:
        return jnp.stack([places(n, o) for o in color_orders(n)])
    return jnp.zeros((2, 16), jnp.int32) + jnp.arange(16, dtype=jnp.int32)


def grad_shapes(width, total):
    cut = split_of(total)
    return [sds((width // 2, c), BF) for c in (cut, cut, total - cut, total - cut)]


def scatter_of(outs, width, n):
    keep0, send0, keep1, send1 = outs
    keep, send = [keep0, keep1], [send0, send1]
    if (width // n) % 16:
        orders = color_orders(n)
        for at in range(2):
            whole = jnp.concatenate([keep[at], send[at]], axis=0).reshape(n, width // n, -1)
            whole = whole[owners(n, orders[at])].reshape(width, -1)
            keep[at], send[at] = whole[: width // 2], whole[width // 2 :]
    return Scatter(keep, send, n)


def mlp_up(source, pos, own, other, routed, upstream, gate, vec, hidden, n):
    ids, halves = source
    rows, width = routed.shape
    outs = [
        sds((rows, width), F32), sds((rows, width), BF), sds((rows, hidden), F32),
        sds((rows, hidden), BF), sds((rows, width), BF),
    ]
    result = call(
        mlp_up_kernel, outs + grad_shapes(width, hidden), [HB, VM, HB, HB, VM] + [VM] * 4,
        (ids, pos, own, other, routed, vec, gate, upstream, *halves), [SM] * 2 + [VM] * 6 + [ANY] * 4,
        [like((rows, width), F32), like((rows, hidden), F32), like((rows, hidden)), like((width, hidden))],
        2 * ids.shape[1] + 16, "mlp_up", LIMITS[1],
    )
    return result[:5], scatter_of(result[5:], width, n)


def mlp_back_kernel(
    idu, idd, dm, slope_hbm, u0, u1, u2, u3, d0, d1, d2, d3, du, part, slope, wu, wd, sem
):
    move = Mover(sem)
    step = 512
    down = move.weights(idd, (d0, d1, d2, d3), wd)
    tiles = [
        move.start(slope_hbm.at[:, pl.ds(at, step)], slope.at[:, pl.ds(at, step)])
        for at in range(0, wd.shape[1], step)
    ]
    up = move.weights(idu, (u0, u1, u2, u3), wu)
    wait(down)
    for at in range(0, wd.shape[1], step):
        dz = nn(dm[...], wd[:, at : at + step])
        tiles[at // step].wait()
        du[:, at : at + step] = (dz * slope[:, at : at + step]).astype(BF)
    wait(up)
    part[...] = nt(du[...], wu[...]).astype(BF)


def mlp_back(up, down, dm, slope):
    rows, width = dm.shape
    hidden = slope.shape[1]
    return call(
        mlp_back_kernel, [sds((rows, hidden), BF), sds((rows, width), BF)], [VM, VM],
        (up[0], down[0], dm, slope, *up[1], *down[1]), [SM, SM, VM, HB] + [ANY] * 8,
        [like((rows, hidden), F32)] + [like((width, hidden))] * 2,
        4 * up[0].shape[1] + 8, "mlp_back", LIMITS[2],
    )


def grad_up_kernel(pos, n2, du, k0, d0, k1, d1, sem):
    cut = k0.shape[1]
    grad_into(pos, [[n2], [n2]], [[du[:, :cut]], [du[:, cut:]]], (k0, d0, k1, d1))


def grad_up(pos, n2, du, n):
    width = n2.shape[1]
    hidden = du.shape[1]
    result = call(
        grad_up_kernel, grad_shapes(width, hidden), [VM] * 4,
        (pos, n2, du), [SM, VM, VM], [], 1, "grad_up", LIMITS[3],
    )
    return scatter_of(result, width, n)


def mlp_out_kernel(idd, dn1, z_hbm, d0, d1, d2, d3, both, z, wd, sem):
    move = Mover(sem)
    first = move.start(z_hbm, z)
    copies = move.weights(idd, (d0, d1, d2, d3), wd)
    rows = dn1.shape[0]
    both[rows:] = dn1[...]
    wait(copies)
    first.wait()
    both[:rows] = nt(z[...], wd[...]).astype(BF)


def mlp_out(down, z, dn1):
    rows, hidden = z.shape
    width = dn1.shape[1]
    return call(
        mlp_out_kernel, sds((2 * rows, width), BF), VM,
        (down[0], dn1, z, *down[1]), [SM, VM, HB] + [ANY] * 4,
        [like((rows, hidden)), like((width, hidden))],
        2 * down[0].shape[1] + 8, "mlp_out", LIMITS[4],
    )


def attn_back_kernel(
    ids, pos, own, other, vec, gate, g, qkv, n1, o, h_hbm, p_hbm, s0, s1, s2, s3,
    dh_hbm, part, gain_out, k0, d0, k1, d1, h, prob, dh, weights, da, do_ref, dqkv, sem,
):
    move = Mover(sem)
    early = move.start(h_hbm, h)
    copies = move.weights(ids, (s0, s1, s2, s3), weights)
    heads_in = move.start(p_hbm, prob)
    rows = h.shape[0]
    w = do_ref.shape[1]
    dn2 = own[rows:].astype(F32) + other[rows:].astype(F32)
    early.wait()
    inverse = lax.rsqrt(jnp.mean(h[...] * h[...], axis=-1, keepdims=True) + epsilon)
    normal = h[...] * inverse
    product = dn2 * normal
    gain_out[...] = jnp.broadcast_to(jnp.sum(product, axis=0, keepdims=True), gain_out.shape)
    gain = vec[1:2]
    dh[...] = inverse * (dn2 * gain - normal * jnp.mean(product * gain, axis=-1, keepdims=True))
    move.put(dh, dh_hbm)
    da[...] = (gate[:, :1] * g[...].astype(F32) + dh[...]).astype(BF)
    wait(copies)
    do_ref[...] = nn(da[...], weights[:, 3 * w : 4 * w]).astype(BF)
    heads_in.wait()
    first = lax.broadcasted_iota(jnp.int32, (CAP, 2 * HD), 1) < HD
    scale = HD**-0.5
    pairs = w // (2 * HD)
    for s in range(rows // CAP):
        at_rows = slice(s * CAP, (s + 1) * CAP)
        for pair in range(pairs):
            at = pair * 2 * HD
            q = qkv[at_rows, at : at + 2 * HD]
            k = qkv[at_rows, w + at : w + at + 2 * HD]
            v = qkv[at_rows, 2 * w + at : 2 * w + at + 2 * HD]
            do = do_ref[at_rows, at : at + 2 * HD]
            zero = jnp.zeros_like(q)
            results = []
            for head in range(2):
                do_one = jnp.where(first, do, zero) if head == 0 else jnp.where(first, zero, do)
                probability = prob[2 * (s * pairs + pair) + head]
                d_probability = nt(do_one, v)
                dv = tn(probability.astype(BF), do)
                inner = jnp.sum(probability * d_probability, axis=-1, keepdims=True)
                ds = (probability * (d_probability - inner)).astype(BF)
                results.append((nn(ds, k) * scale, tn(ds, q) * scale, dv))
            for which in range(3):
                value = jnp.where(first, results[0][which], results[1][which]).astype(BF)
                dqkv[at_rows, which * w + at : which * w + at + 2 * HD] = value
    cut = k0.shape[1]
    grad_into(pos, [[n1], [n1, da]], [[dqkv[:, :cut]], [dqkv[:, cut:], o[...]]], (k0, d0, k1, d1))
    part[...] = nt(dqkv[...], weights[:, : 3 * w]).astype(BF)
    move.finish()


def attn_back(source, pos, own, other, h, vec, upstream, gate, qkv, prob, n1, attended, n):
    ids, halves = source
    rows, width = h.shape
    w = attended.shape[1]
    outs = [sds((rows, width), F32), sds((rows, width), BF), sds((8, width), F32)]
    result = call(
        attn_back_kernel, outs + grad_shapes(width, 4 * w), [HB, VM, VM] + [VM] * 4,
        (ids, pos, own, other, vec, gate, upstream, qkv, n1, attended, h, prob, *halves),
        [SM] * 2 + [VM] * 8 + [HB] * 2 + [ANY] * 4,
        [
            like((rows, width), F32), like(prob.shape, F32), like((rows, width), F32),
            like((width, 4 * w + EXTRA)), like((rows, width)), like((rows, w)), like((rows, 3 * w)),
        ],
        2 * ids.shape[1] + 8, "attn_back", LIMITS[5],
    )
    return result[:3], scatter_of(result[3:], width, n)


TILE = 1024


def select_rows(slot_ref, sel, rows, x_ref, out_ref):
    place = lax.broadcasted_iota(jnp.int32, (CAP, LANE), 0).astype(F32)
    for at in range(TILE // LANE):
        sel[:, at * LANE : (at + 1) * LANE] = jnp.where(place == slot_ref[at], 1.0, 0.0).astype(BF)
    put = tn(sel[...], rows[...])
    hit = tn(sel[...], jnp.ones((CAP, LANE), BF))[:, :1]
    out_ref[...] = jnp.where(hit > 0.5, put.astype(BF), x_ref[...])


def place_kernel(slot_ref, x_ref, rows, out_ref, sel):
    select_rows(slot_ref, sel, rows, x_ref, out_ref)


def place_rows(slot, tokens, rows, name):
    width = tokens.shape[1]
    per = LEN // TILE
    seqs = tokens.shape[0] // LEN
    groups = TILE // LANE
    return pl.pallas_call(
        place_kernel,
        grid=(seqs, per),
        in_specs=[
            pl.BlockSpec((groups, 1, LANE), lambda s, t: (s * per + t, 0, 0)),
            pl.BlockSpec((TILE, width), lambda s, t: (s * per + t, 0)),
            pl.BlockSpec((CAP, width), lambda s, t: (s, 0)),
        ],
        out_specs=pl.BlockSpec((TILE, width), lambda s, t: (s * per + t, 0)),
        out_shape=sds(tokens.shape, BF),
        scratch_shapes=[pltpu.VMEM((CAP, TILE), BF)],
        compiler_params=pltpu.CompilerParams(vmem_limit_bytes=LIMITS[6] * MIB),
        cost_estimate=COST,
        name=name,
    )(slot, tokens, rows)


def rows_kernel(
    count_ref, both_own, both_other, dn1_own, dn1_other, attn_own_any, attn_other_any, r_any, g_any, gate_any, vec_any, dh_any,
    out_ref, back_ref, small_ref, attn_own, attn_other, r, g, gate_ref, vec, dh, sem,
):
    move = Mover(sem)
    pairs = (
        (r_any, r), (g_any, g), (attn_own_any, attn_own), (attn_other_any, attn_other),
        (gate_any, gate_ref), (vec_any, vec), (dh_any, dh),
    )
    copies = [move.start(src, dst) for src, dst in pairs]
    rows = r.shape[0]
    wait(copies)
    inputs = r[...].astype(F32)
    upstream = g[...].astype(F32)
    gate = gate_ref[:, :1]
    attention = attn_own[...].astype(F32) + attn_other[...].astype(F32)
    branch = attention + (both_own[:rows].astype(F32) + both_other[:rows].astype(F32))
    out_ref[...] = (inputs + gate * branch).astype(BF)
    dl = jnp.sum(upstream * branch, axis=-1, keepdims=True) * gate * (1.0 - gate)
    d_router = jnp.sum(dl * inputs, axis=0, keepdims=True)
    dn1 = dn1_own[...].astype(F32) + dn1_other[...].astype(F32)
    inverse = lax.rsqrt(jnp.mean(inputs * inputs, axis=-1, keepdims=True) + epsilon)
    normal = inputs * inverse
    product = dn1 * normal
    d_gain = jnp.sum(product, axis=0, keepdims=True)
    gain = vec[0:1]
    dr = inverse * (dn1 * gain - normal * jnp.mean(product * gain, axis=-1, keepdims=True))
    back_ref[...] = (upstream + dh[...] + dl * vec[2:3] + dr).astype(BF)
    row = lax.broadcasted_iota(jnp.int32, (CAP, LANE), 0)
    total = jnp.zeros((1, LANE), F32)
    for s in range(rows // CAP):
        part = gate_ref[s * CAP : (s + 1) * CAP]
        total += jnp.sum(jnp.where(row < count_ref[s], part, 0.0), axis=0, keepdims=True)
    small_ref[0:1] = d_gain
    small_ref[1:2] = d_router
    small_ref[2:3] = jnp.concatenate([total] * (d_gain.shape[1] // LANE), axis=1)
    small_ref[3:8] = jnp.zeros((5, d_gain.shape[1]), F32)


def rows_last(counts, attn_own, attn_other, both_own, both_other, dn1_own, dn1_other, routed, upstream, gate, vec, dh):
    rows, width = routed.shape
    ins = (attn_own, attn_other, routed, upstream, gate, vec, dh)
    return call(
        rows_kernel,
        [sds((rows, width), BF), sds((rows, width), BF), sds((8, width), F32)], [VM] * 3,
        (counts, both_own, both_other, dn1_own, dn1_other, *ins), [SM] + [VM] * 4 + [ANY] * len(ins),
        [like(x.shape, x.dtype) for x in ins], len(ins), "rows_last", LIMITS[8],
    )


def body(
    tokens_in,
    route_mask,
    cotangent,
    w_query,
    w_key,
    w_value,
    w_out,
    w_up,
    w_down,
    gain_attn,
    gain_mlp,
    router,
):
    n = lax.axis_size("dp")
    mine, w = w_query.shape
    hidden = w_up.shape[1]
    width = tokens_in.shape[1]
    seqs = tokens_in.shape[0] // LEN
    extras = jnp.concatenate(
        [gain_attn[:, None], gain_mlp[:, None], router[:, None], jnp.zeros((mine, EXTRA - 3), BF)], axis=1
    )
    attn = Gather(jnp.concatenate([w_query, w_key, w_value, w_out.T, extras], axis=1), n)
    up = Gather(w_up, n)
    down = Gather(w_down.T, n)
    counts = jnp.sum(route_mask.reshape(seqs, LEN), axis=1).astype(jnp.int32)

    def start(chains, token, swaps=()):
        held = [c.held if isinstance(c, Gather) else c.send for c in chains]
        flat = tie([v for h in held for v in h] + list(swaps), token)
        arrived = []
        for chain, h in zip(chains, held):
            part, flat = flat[: len(h)], flat[len(h) :]
            if isinstance(chain, Gather):
                chain.held = part
            else:
                chain.send = part
            arrived += chain.begin()
        swapped = [other_core(v) for v in flat]
        return arrived + swapped, swapped

    def close(chains, made=()):
        flat = tie([g for c in chains for g in c.got], made)
        for chain in chains:
            chain.got, flat = flat[: len(chain.got)], flat[len(chain.got) :]
            chain.end()

    pos = places_of(width, n)
    four = attn.steps == 4

    token, _ = start([attn], [])
    routed, upstream, slot = pick(route_mask, tokens_in, cotangent, seqs)
    close([attn], [slot])
    for chains in ([attn, up], [attn, up], [attn, down]) if four else [[attn, up, down]] * (attn.steps - 1):
        token, _ = start(chains, token)
        close(chains)
    src_attn = attn.result()
    rest = [[up, down], [up, down], [down]] if four else [[up, down], [], []]
    token, _ = start(rest[0], token)
    n1, qkv, attended, attn_own, gate, vec, prob = attn_fwd(src_attn, counts, routed, w)
    close(rest[0], [attn_own])
    token, (attn_other,) = start(rest[1], token, [attn_own])
    close(rest[1])
    src_up = up.result()
    token, _ = start(rest[2], token)
    (h, n2, slope, z, dm), sum_down = mlp_up(
        src_up, pos, attn_own, attn_other, routed, upstream, gate, vec, hidden, n
    )
    close(rest[2], [dm])
    src_down = down.result()

    token, _ = start([sum_down], token)
    du, dn2_own = mlp_back(src_up, src_down, dm, slope)
    both_own = mlp_out(src_down, z, dn2_own)
    sum_up = grad_up(pos, n2, du, n)
    close([sum_down], sum_up.send + [both_own])
    token, (both_other,) = start([sum_up, sum_down], token, [both_own])
    (dh, dn1_own, gain_two), sum_attn = attn_back(
        src_attn, pos, both_own, both_other, h, vec, upstream, gate, qkv, prob, n1, attended, n
    )
    close([sum_up, sum_down], [gain_two])
    token, (dn1_other,) = start([sum_attn, sum_down], token, [dn1_own])
    down_there = token[-3:-1]
    close([sum_down])
    more, _ = start([sum_up], down_there)
    out_rows, back_rows, sums = rows_last(
        counts, attn_own, attn_other, both_own, both_other, dn1_own, dn1_other, routed, upstream, gate, vec, dh
    )
    block_out = place_rows(slot, tokens_in, out_rows, "place_out")
    close([sum_attn, sum_up], [block_out])
    token = token + more
    token, _ = start([sum_attn, sum_up, sum_down], token)
    (back_late,) = tie([back_rows], [token[0]])
    input_grad = place_rows(slot, cotangent, back_late, "place_grad")
    close([sum_attn, sum_up, sum_down], [input_grad])
    live = [c for c in (sum_attn, sum_up, sum_down) if c.at]
    scalars = jnp.stack([jnp.sum(counts).astype(F32), sums[2, 0]])
    small = jnp.concatenate(
        [
            sums[0].reshape(n, mine),
            gain_two[0].reshape(n, mine),
            sums[1].reshape(n, mine),
            jnp.broadcast_to(scalars, (n, 2)),
        ],
        axis=1,
    )
    (small,) = tie([small], [input_grad])
    small = lax.all_to_all(small, "dp", 0, 0, tiled=True)
    while live:
        token, _ = start(live, token)
        close(live)
        live = [c for c in live if c.at]
    small = jnp.sum(small, axis=0)
    total_attn, total_up, total_down = sum_attn.result(), sum_up.result(), sum_down.result()
    token_total = tokens_in.shape[0] * n
    return (
        block_out,
        input_grad,
        total_attn[:, :w],
        total_attn[:, w : 2 * w],
        total_attn[:, 2 * w : 3 * w],
        total_attn[:, 3 * w :].T,
        total_up,
        total_down.T,
        small[:mine],
        small[mine : 2 * mine],
        small[2 * mine : 3 * mine],
        small[3 * mine] / token_total,
        small[3 * mine + 1] / small[3 * mine],
    )


def solution(mesh):
    rows, cols = P("dp", "mp"), P("mp", "dp")
    return jax.shard_map(
        body,
        mesh=mesh,
        in_specs=(P("dp", None), P("dp"), P("dp", None), rows, rows, rows, cols, rows, cols) + (P("dp"),) * 3,
        out_specs=(P("dp", None), P("dp", None), rows, rows, rows, cols, rows, cols) + (P("dp"),) * 3 + (P(), P()),
        check_vma=False,
    )
```

```python
import jax
import jax.numpy as jnp
from jax import lax
from jax.experimental import pallas as pl
from jax.experimental.pallas import tpu as pltpu
from jax.sharding import PartitionSpec as P

HD = 64
LEN = 2048
CAP = 256
LANE = 128
EXTRA = 128
MIB = 1 << 20
LIMITS = (20, 28, 24, 12, 14, 34, 24, 46, 24)
FAR = 12
COST = pl.CostEstimate(flops=8000000000, bytes_accessed=24000000, transcendentals=0)

epsilon = 1e-06
negative = -1e30
BF = jnp.bfloat16
F32 = jnp.float32
SM = pl.BlockSpec(memory_space=pltpu.SMEM)
HB = pl.BlockSpec(memory_space=pltpu.HBM)
VM = pl.BlockSpec(memory_space=pltpu.VMEM)
ANY = pl.BlockSpec(memory_space=pl.ANY)


def nn(a, b):
    return jnp.dot(a, b, preferred_element_type=F32)


def nt(a, b):
    return lax.dot_general(a, b, (((1,), (1,)), ((), ())), preferred_element_type=F32)


def tn(a, b):
    return lax.dot_general(a, b, (((0,), (0,)), ((), ())), preferred_element_type=F32)


def sds(shape, dtype):
    return jax.ShapeDtypeStruct(shape, dtype)


def color_orders(n):
    bits = n.bit_length() - 1
    if bits == 4:
        x, y, z1, z2 = 1, 2, 4, 8
        return (((z2, y, z1, x), (z2, z1, x, y)), ((z2, x, y, z1), (z2, x, y, z1)))
    down = tuple(1 << b for b in reversed(range(bits)))
    return ((down, down), (down, down))


def bit_sum(n, index, source, target):
    total = jnp.zeros((n,), jnp.int32)
    for one, two in zip(source, target):
        total = total | jnp.where((index & one) != 0, two, 0)
    return total


def spots(orders):
    return [1 << k for k in range(len(orders[0]))]


def owners(n, orders):
    p = jnp.arange(n, dtype=jnp.int32)
    one, two = (bit_sum(n, p, spots(orders), o) for o in orders)
    return lax.axis_index("dp") ^ jnp.where(lax.axis_index("mp") == 0, one, two)


def places(n, orders):
    d = jnp.arange(n, dtype=jnp.int32) ^ lax.axis_index("dp")
    one, two = (bit_sum(n, d, o, spots(orders)) for o in orders)
    return jnp.where(lax.axis_index("mp") == 0, one, two)


def hop(array, n, one, two):
    pairs = [(d * 2 + c, (d ^ (one, two)[c]) * 2 + c) for d in range(n) for c in range(2)]
    return lax.ppermute(array, ("dp", "mp"), pairs)


def other_core(array):
    return lax.ppermute(array, "mp", [(0, 1), (1, 0)])


def split_of(width):
    return -(-width * 2 // (3 * LANE)) * LANE


class Gather:
    def __init__(self, shard, n):
        self.n = n
        self.orders = color_orders(n)
        self.steps = len(self.orders[0][0])
        self.at = 0
        self.width = shard.shape[1]
        self.cut = split_of(self.width)
        self.held = [shard]
        self.got = None

    def begin(self):
        k = self.at
        if k == 0:
            one, two = self.orders[0][0][0], self.orders[0][1][0]
            self.got = [hop(self.held[0], self.n, one, two)]
        else:
            self.got = [hop(h, self.n, o[0][k], o[1][k]) for h, o in zip(self.held, self.orders)]
        self.at += 1
        return self.got

    def end(self):
        if self.at == self.steps:
            return
        if self.at == 1:
            both = jnp.concatenate([self.held[0], self.got[0]], axis=0)
            self.held = [both[:, : self.cut], both[:, self.cut :]]
        else:
            self.held = [jnp.concatenate([h, g], axis=0) for h, g in zip(self.held, self.got)]

    def result(self):
        n = self.n
        ids = jnp.stack([owners(n, o) for o in self.orders])
        halves = [self.held[0], self.got[0], self.held[1], self.got[1]]
        rows = 2 * self.held[0].shape[0]
        if (rows // n) % 16:
            out = []
            for at, (h, g) in enumerate(zip(self.held, self.got)):
                blocks = jnp.concatenate([h, g], axis=0).reshape(n, rows // n, -1)
                blocks = blocks[places(n, self.orders[at])].reshape(rows, -1)
                out += [blocks[: rows // 2], blocks[rows // 2 :]]
            return jnp.zeros((2, 2), jnp.int32) + jnp.arange(2, dtype=jnp.int32), out
        return ids, halves


class Scatter:
    def __init__(self, keep, send, n):
        self.n = n
        self.orders = color_orders(n)
        self.steps = len(self.orders[0][0])
        self.at = self.steps
        self.keep, self.send = keep, send

    def ops(self):
        return self.send

    def begin(self):
        k = self.at - 1
        if len(self.send) == 1:
            one, two = self.orders[0][0][0], self.orders[0][1][0]
            self.got = [hop(self.send[0], self.n, one, two)]
        else:
            self.got = [hop(s, self.n, o[0][k], o[1][k]) for s, o in zip(self.send, self.orders)]
        self.at -= 1
        return self.got

    def end(self):
        half = self.got[0].shape[0] // 2
        if self.at == 0:
            self.keep = [k.astype(F32) + g.astype(F32) for k, g in zip(self.keep, self.got)]
            self.send = []
            return
        send = [(k[half:].astype(F32) + g[half:].astype(F32)).astype(BF) for k, g in zip(self.keep, self.got)]
        keep = [(k[:half].astype(F32) + g[:half].astype(F32)).astype(BF) for k, g in zip(self.keep, self.got)]
        if self.at == 1:
            keep = [jnp.concatenate(keep, axis=1)]
            send = [jnp.concatenate(send, axis=1)]
        self.keep, self.send = keep, send

    def result(self):
        return self.keep[0]


def tie(values, tokens):
    if not tokens:
        return list(values)
    out = lax.optimization_barrier(tuple(values) + tuple(tokens))
    return list(out[: len(values)])


def pick_kernel(mask_ref, x_ref, c_ref, r_ref, g_ref, slot_ref, sel):
    groups = mask_ref.shape[1]
    flag = mask_ref[0].astype(F32)
    up = lax.broadcasted_iota(jnp.int32, (LANE, LANE), 0) <= lax.broadcasted_iota(jnp.int32, (LANE, LANE), 1)
    within = nn(flag, up.astype(F32))
    total = jnp.broadcast_to(within[:, LANE - 1 :], (groups, LANE))
    low = lax.broadcasted_iota(jnp.int32, (groups, groups), 1) < lax.broadcasted_iota(
        jnp.int32, (groups, groups), 0
    )
    rank = within + nn(low.astype(F32), total) - 1.0
    slot = jnp.where(flag > 0, rank, -1.0)
    place = lax.broadcasted_iota(jnp.int32, (CAP, LANE), 0).astype(F32)
    for at in range(groups):
        slot_ref[at] = slot[at : at + 1]
        sel[:, at * LANE : (at + 1) * LANE] = jnp.where(place == slot[at : at + 1], 1.0, 0.0).astype(BF)
    r_ref[...] = nn(sel[...], x_ref[...]).astype(BF)
    g_ref[...] = nn(sel[...], c_ref[...]).astype(BF)


def pick(mask, tokens, cotangent, seqs):
    width = tokens.shape[1]
    groups = LEN // LANE
    return pl.pallas_call(
        pick_kernel,
        grid=(seqs,),
        in_specs=[
            pl.BlockSpec((1, groups, LANE), lambda s: (s, 0, 0)),
            pl.BlockSpec((LEN, width), lambda s: (s, 0)),
            pl.BlockSpec((LEN, width), lambda s: (s, 0)),
        ],
        out_specs=[
            pl.BlockSpec((CAP, width), lambda s: (s, 0)),
            pl.BlockSpec((CAP, width), lambda s: (s, 0)),
            pl.BlockSpec((groups, 1, LANE), lambda s: (s, 0, 0)),
        ],
        out_shape=[
            sds((seqs * CAP, width), BF),
            sds((seqs * CAP, width), BF),
            sds((seqs * groups, 1, LANE), F32),
        ],
        scratch_shapes=[pltpu.VMEM((CAP, LEN), BF)],
        compiler_params=pltpu.CompilerParams(vmem_limit_bytes=LIMITS[7] * MIB),
        cost_estimate=COST,
        name="pick",
    )(mask.reshape(seqs, groups, LANE), tokens, cotangent)


class Mover:
    def __init__(self, sem):
        self.sem = sem
        self.used = 0
        self.out = []

    def start(self, src, dst):
        copy = pltpu.make_async_copy(src, dst, self.sem.at[self.used])
        self.used += 1
        copy.start()
        return copy

    def put(self, src, dst):
        self.out.append(self.start(src, dst))

    def weights(self, ids_ref, halves, dst):
        blocks = ids_ref.shape[1]
        rows = dst.shape[0] // blocks
        copies = []
        col = 0
        for piece in range(2):
            width = halves[2 * piece].shape[1]
            for at in range(blocks):
                src = halves[2 * piece + at // (blocks // 2)]
                from_row = (at % (blocks // 2)) * rows
                to_row = pl.multiple_of(ids_ref[piece, at] * rows, rows)
                copies.append(
                    self.start(src.at[pl.ds(from_row, rows), :], dst.at[pl.ds(to_row, rows), pl.ds(col, width)])
                )
            col += width
        return copies

    def finish(self):
        wait(self.out)


def wait(copies):
    for copy in copies:
        copy.wait()


def like(shape, dtype=BF):
    return pltpu.VMEM(shape, dtype)


def call(kernel, out_shape, out_specs, args, in_specs, scratch, copies, name, limit):
    return pl.pallas_call(
        kernel,
        out_shape=out_shape,
        in_specs=in_specs,
        out_specs=out_specs,
        scratch_shapes=list(scratch) + [pltpu.SemaphoreType.DMA((copies,))],
        compiler_params=pltpu.CompilerParams(vmem_limit_bytes=limit * MIB),
        cost_estimate=COST,
        name=name,
    )(*args)


def softmax(queries, keys, allowed):
    scores = nt(queries, keys) * (HD**-0.5)
    scores = jnp.where(allowed, scores, negative)
    raised = jnp.exp(scores - jnp.max(scores, axis=-1, keepdims=True))
    return raised / jnp.sum(raised, axis=-1, keepdims=True)


def allowed_slots(count):
    row = lax.broadcasted_iota(jnp.int32, (CAP, CAP), 0)
    col = lax.broadcasted_iota(jnp.int32, (CAP, CAP), 1)
    return (col <= row) & (col < count)


def attn_fwd_kernel(
    ids, count_ref, r, s0, s1, s2, s3, n1, qkv, o, part, gate, vec, p_hbm, weights, prob, sem
):
    move = Mover(sem)
    copies = move.weights(ids, (s0, s1, s2, s3), weights)
    w = o.shape[1]
    seqs = r.shape[0] // CAP
    inputs = r[...].astype(F32)
    normal = inputs * lax.rsqrt(jnp.mean(inputs * inputs, axis=-1, keepdims=True) + epsilon)
    wait(copies)
    vectors = weights[:, 4 * w :].astype(F32).T[:8]
    vec[...] = vectors
    n1[...] = (normal * vectors[0:1]).astype(BF)
    logit = jnp.sum(inputs * vectors[2:3], axis=-1, keepdims=True)
    gate[...] = jnp.broadcast_to(jax.nn.sigmoid(logit), gate.shape)
    qkv[...] = nn(n1[...], weights[:, : 3 * w]).astype(BF)
    first = lax.broadcasted_iota(jnp.int32, (CAP, 2 * HD), 1) < HD
    pairs = w // (2 * HD)
    for s in range(seqs):
        allowed = allowed_slots(count_ref[s])
        rows = slice(s * CAP, (s + 1) * CAP)
        for pair in range(pairs):
            at = pair * 2 * HD
            q = qkv[rows, at : at + 2 * HD]
            k = qkv[rows, w + at : w + at + 2 * HD]
            v = qkv[rows, 2 * w + at : 2 * w + at + 2 * HD]
            zero = jnp.zeros_like(q)
            one = softmax(jnp.where(first, q, zero), k, allowed)
            two = softmax(jnp.where(first, zero, q), k, allowed)
            head = 2 * (s * pairs + pair)
            prob[head] = one
            prob[head + 1] = two
            o[rows, at : at + 2 * HD] = jnp.where(first, nn(one.astype(BF), v), nn(two.astype(BF), v)).astype(BF)
        half = pl.ds(2 * s * pairs, 2 * pairs)
        move.put(prob.at[half], p_hbm.at[half])
    part[...] = nt(o[...], weights[:, 3 * w : 4 * w]).astype(BF)
    move.finish()


def attn_fwd(source, counts, routed, w):
    ids, halves = source
    rows, width = routed.shape
    heads = rows // CAP * w // HD
    outs = [
        sds((rows, width), BF), sds((rows, 3 * w), BF), sds((rows, w), BF), sds((rows, width), BF),
        sds((rows, LANE), F32), sds((8, width), F32), sds((FAR * heads, CAP, CAP), F32),
    ]
    return call(
        attn_fwd_kernel, outs, [VM] * 6 + [HB],
        (ids, counts, routed, *halves), [SM, SM, VM] + [ANY] * 4,
        [like((width, 4 * w + EXTRA)), like((heads, CAP, CAP), F32)],
        2 * ids.shape[1] + 4, "attn_fwd", LIMITS[0],
    )


def grad_into(pos, lefts, rights, outs):
    blocks = pos.shape[1]
    width = 2 * outs[0].shape[0]
    rows = width // blocks
    tile = 256
    for at in range(0, width, tile):
        for piece in range(2):
            keep, send = outs[2 * piece], outs[2 * piece + 1]
            col = 0
            for left, right in zip(lefts[piece], rights[piece]):
                value = tn(left[:, at : at + tile], right).astype(BF)
                cols = slice(col, col + right.shape[1])
                col += right.shape[1]
                for b in range(0, tile, rows):
                    place = pos[piece, (at + b) // rows]
                    block = value[b : b + rows]

                    @pl.when(place < blocks // 2)
                    def _():
                        keep[pl.ds(pl.multiple_of(place * rows, rows), rows), cols] = block

                    @pl.when(place >= blocks // 2)
                    def _():
                        send[pl.ds(pl.multiple_of((place - blocks // 2) * rows, rows), rows), cols] = block


def mlp_up_kernel(
    ids, pos, own, other, r, vec, gate, g, s0, s1, s2, s3,
    h_hbm, n2, slope_hbm, z_hbm, dm, k0, d0, k1, d1, h, slope, z, weights, sem,
):
    move = Mover(sem)
    copies = move.weights(ids, (s0, s1, s2, s3), weights)
    h[...] = r[...].astype(F32) + (own[...].astype(F32) + other[...].astype(F32))
    move.put(h, h_hbm)
    normal = h[...] * lax.rsqrt(jnp.mean(h[...] * h[...], axis=-1, keepdims=True) + epsilon)
    n2[...] = (normal * vec[1:2]).astype(BF)
    dm[...] = (gate[:, :1] * g[...].astype(F32)).astype(BF)
    wait(copies)
    a, c = 0.044715, 0.7978845608028654
    step = 512
    for at in range(0, weights.shape[1], step):
        cols = slice(at, at + step)
        u = nn(n2[...], weights[:, cols])
        square = u * u
        t = jnp.tanh(c * (u + a * (square * u)))
        half = 0.5 * (1.0 + t)
        z[:, cols] = (u * half).astype(BF)
        slope[:, cols] = half + 0.5 * u * (1.0 - t * t) * (c * (1.0 + 3.0 * a * square))
        move.put(slope.at[:, pl.ds(at, step)], slope_hbm.at[pl.ds(0, slope.shape[0]), pl.ds(at, step)])
    move.put(z, z_hbm)
    cut = k0.shape[1]
    grad_into(pos, [[dm], [dm]], [[z[:, :cut]], [z[:, cut:]]], (k0, d0, k1, d1))
    move.finish()


def places_of(width, n):
    if (width // n) % 16 == 0:
        return jnp.stack([places(n, o) for o in color_orders(n)])
    return jnp.zeros((2, 16), jnp.int32) + jnp.arange(16, dtype=jnp.int32)


def grad_shapes(width, total):
    cut = split_of(total)
    return [sds((width // 2, c), BF) for c in (cut, cut, total - cut, total - cut)]


def scatter_of(outs, width, n):
    keep0, send0, keep1, send1 = outs
    keep, send = [keep0, keep1], [send0, send1]
    if (width // n) % 16:
        orders = color_orders(n)
        for at in range(2):
            whole = jnp.concatenate([keep[at], send[at]], axis=0).reshape(n, width // n, -1)
            whole = whole[owners(n, orders[at])].reshape(width, -1)
            keep[at], send[at] = whole[: width // 2], whole[width // 2 :]
    return Scatter(keep, send, n)


def mlp_up(source, pos, own, other, routed, upstream, gate, vec, hidden, n):
    ids, halves = source
    rows, width = routed.shape
    outs = [
        sds((rows, width), F32), sds((rows, width), BF), sds((FAR * rows, hidden), F32),
        sds((rows, hidden), BF), sds((rows, width), BF),
    ]
    result = call(
        mlp_up_kernel, outs + grad_shapes(width, hidden), [HB, VM, HB, HB, VM] + [VM] * 4,
        (ids, pos, own, other, routed, vec, gate, upstream, *halves), [SM] * 2 + [VM] * 6 + [ANY] * 4,
        [like((rows, width), F32), like((rows, hidden), F32), like((rows, hidden)), like((width, hidden))],
        2 * ids.shape[1] + 16, "mlp_up", LIMITS[1],
    )
    return result[:5], scatter_of(result[5:], width, n)


def mlp_back_kernel(
    idu, idd, dm, slope_hbm, u0, u1, u2, u3, d0, d1, d2, d3, du, part, slope, wu, wd, sem
):
    move = Mover(sem)
    step = 512
    down = move.weights(idd, (d0, d1, d2, d3), wd)
    tiles = [
        move.start(slope_hbm.at[pl.ds(0, slope.shape[0]), pl.ds(at, step)], slope.at[:, pl.ds(at, step)])
        for at in range(0, wd.shape[1], step)
    ]
    up = move.weights(idu, (u0, u1, u2, u3), wu)
    wait(down)
    for at in range(0, wd.shape[1], step):
        dz = nn(dm[...], wd[:, at : at + step])
        tiles[at // step].wait()
        du[:, at : at + step] = (dz * slope[:, at : at + step]).astype(BF)
    wait(up)
    part[...] = nt(du[...], wu[...]).astype(BF)


def mlp_back(up, down, dm, slope):
    rows, width = dm.shape
    hidden = slope.shape[1]
    return call(
        mlp_back_kernel, [sds((rows, hidden), BF), sds((rows, width), BF)], [VM, VM],
        (up[0], down[0], dm, slope, *up[1], *down[1]), [SM, SM, VM, HB] + [ANY] * 8,
        [like((rows, hidden), F32)] + [like((width, hidden))] * 2,
        4 * up[0].shape[1] + 8, "mlp_back", LIMITS[2],
    )


def grad_up_kernel(pos, n2, du, k0, d0, k1, d1, sem):
    cut = k0.shape[1]
    grad_into(pos, [[n2], [n2]], [[du[:, :cut]], [du[:, cut:]]], (k0, d0, k1, d1))


def grad_up(pos, n2, du, n):
    width = n2.shape[1]
    hidden = du.shape[1]
    result = call(
        grad_up_kernel, grad_shapes(width, hidden), [VM] * 4,
        (pos, n2, du), [SM, VM, VM], [], 1, "grad_up", LIMITS[3],
    )
    return scatter_of(result, width, n)


def mlp_out_kernel(idd, dn1, z_hbm, d0, d1, d2, d3, both, z, wd, sem):
    move = Mover(sem)
    first = move.start(z_hbm, z)
    copies = move.weights(idd, (d0, d1, d2, d3), wd)
    rows = dn1.shape[0]
    both[rows:] = dn1[...]
    wait(copies)
    first.wait()
    both[:rows] = nt(z[...], wd[...]).astype(BF)


def mlp_out(down, z, dn1):
    rows, hidden = z.shape
    width = dn1.shape[1]
    return call(
        mlp_out_kernel, sds((2 * rows, width), BF), VM,
        (down[0], dn1, z, *down[1]), [SM, VM, HB] + [ANY] * 4,
        [like((rows, hidden)), like((width, hidden))],
        2 * down[0].shape[1] + 8, "mlp_out", LIMITS[4],
    )


def attn_back_kernel(
    ids, pos, own, other, vec, gate, g, qkv, n1, o, h_hbm, p_hbm, s0, s1, s2, s3,
    dh_hbm, part, gain_out, k0, d0, k1, d1, h, prob, dh, weights, da, do_ref, dqkv, sem,
):
    move = Mover(sem)
    early = move.start(h_hbm, h)
    copies = move.weights(ids, (s0, s1, s2, s3), weights)
    heads_in = move.start(p_hbm.at[pl.ds(0, prob.shape[0])], prob)
    rows = h.shape[0]
    w = do_ref.shape[1]
    dn2 = own[rows:].astype(F32) + other[rows:].astype(F32)
    early.wait()
    inverse = lax.rsqrt(jnp.mean(h[...] * h[...], axis=-1, keepdims=True) + epsilon)
    normal = h[...] * inverse
    product = dn2 * normal
    gain_out[...] = jnp.broadcast_to(jnp.sum(product, axis=0, keepdims=True), gain_out.shape)
    gain = vec[1:2]
    dh[...] = inverse * (dn2 * gain - normal * jnp.mean(product * gain, axis=-1, keepdims=True))
    move.put(dh, dh_hbm)
    da[...] = (gate[:, :1] * g[...].astype(F32) + dh[...]).astype(BF)
    wait(copies)
    do_ref[...] = nn(da[...], weights[:, 3 * w : 4 * w]).astype(BF)
    heads_in.wait()
    first = lax.broadcasted_iota(jnp.int32, (CAP, 2 * HD), 1) < HD
    scale = HD**-0.5
    pairs = w // (2 * HD)
    for s in range(rows // CAP):
        at_rows = slice(s * CAP, (s + 1) * CAP)
        for pair in range(pairs):
            at = pair * 2 * HD
            q = qkv[at_rows, at : at + 2 * HD]
            k = qkv[at_rows, w + at : w + at + 2 * HD]
            v = qkv[at_rows, 2 * w + at : 2 * w + at + 2 * HD]
            do = do_ref[at_rows, at : at + 2 * HD]
            zero = jnp.zeros_like(q)
            results = []
            for head in range(2):
                do_one = jnp.where(first, do, zero) if head == 0 else jnp.where(first, zero, do)
                probability = prob[2 * (s * pairs + pair) + head]
                d_probability = nt(do_one, v)
                dv = tn(probability.astype(BF), do)
                inner = jnp.sum(probability * d_probability, axis=-1, keepdims=True)
                ds = (probability * (d_probability - inner)).astype(BF)
                results.append((nn(ds, k) * scale, tn(ds, q) * scale, dv))
            for which in range(3):
                value = jnp.where(first, results[0][which], results[1][which]).astype(BF)
                dqkv[at_rows, which * w + at : which * w + at + 2 * HD] = value
    cut = k0.shape[1]
    grad_into(pos, [[n1], [n1, da]], [[dqkv[:, :cut]], [dqkv[:, cut:], o[...]]], (k0, d0, k1, d1))
    part[...] = nt(dqkv[...], weights[:, : 3 * w]).astype(BF)
    move.finish()


def attn_back(source, pos, own, other, h, vec, upstream, gate, qkv, prob, n1, attended, n):
    ids, halves = source
    rows, width = h.shape
    w = attended.shape[1]
    outs = [sds((rows, width), F32), sds((rows, width), BF), sds((8, width), F32)]
    result = call(
        attn_back_kernel, outs + grad_shapes(width, 4 * w), [HB, VM, VM] + [VM] * 4,
        (ids, pos, own, other, vec, gate, upstream, qkv, n1, attended, h, prob, *halves),
        [SM] * 2 + [VM] * 8 + [HB] * 2 + [ANY] * 4,
        [
            like((rows, width), F32), like((prob.shape[0] // FAR, CAP, CAP), F32), like((rows, width), F32),
            like((width, 4 * w + EXTRA)), like((rows, width)), like((rows, w)), like((rows, 3 * w)),
        ],
        2 * ids.shape[1] + 8, "attn_back", LIMITS[5],
    )
    return result[:3], scatter_of(result[3:], width, n)


TILE = 1024


def select_rows(slot_ref, sel, rows, x_ref, out_ref):
    place = lax.broadcasted_iota(jnp.int32, (CAP, LANE), 0).astype(F32)
    for at in range(TILE // LANE):
        sel[:, at * LANE : (at + 1) * LANE] = jnp.where(place == slot_ref[at], 1.0, 0.0).astype(BF)
    put = tn(sel[...], rows[...])
    hit = tn(sel[...], jnp.ones((CAP, LANE), BF))[:, :1]
    out_ref[...] = jnp.where(hit > 0.5, put.astype(BF), x_ref[...])


def place_kernel(slot_ref, x_ref, rows, out_ref, sel):
    select_rows(slot_ref, sel, rows, x_ref, out_ref)


def place_rows(slot, tokens, rows, name):
    width = tokens.shape[1]
    per = LEN // TILE
    seqs = tokens.shape[0] // LEN
    groups = TILE // LANE
    return pl.pallas_call(
        place_kernel,
        grid=(seqs, per),
        in_specs=[
            pl.BlockSpec((groups, 1, LANE), lambda s, t: (s * per + t, 0, 0)),
            pl.BlockSpec((TILE, width), lambda s, t: (s * per + t, 0)),
            pl.BlockSpec((CAP, width), lambda s, t: (s, 0)),
        ],
        out_specs=pl.BlockSpec((TILE, width), lambda s, t: (s * per + t, 0)),
        out_shape=sds(tokens.shape, BF),
        scratch_shapes=[pltpu.VMEM((CAP, TILE), BF)],
        compiler_params=pltpu.CompilerParams(vmem_limit_bytes=LIMITS[6] * MIB),
        cost_estimate=COST,
        name=name,
    )(slot, tokens, rows)


def rows_kernel(
    count_ref, both_own, both_other, dn1_own, dn1_other, attn_own_any, attn_other_any, r_any, g_any, gate_any, vec_any, dh_any,
    out_ref, back_ref, small_ref, attn_own, attn_other, r, g, gate_ref, vec, dh, sem,
):
    move = Mover(sem)
    pairs = (
        (r_any, r), (g_any, g), (attn_own_any, attn_own), (attn_other_any, attn_other),
        (gate_any, gate_ref), (vec_any, vec), (dh_any, dh),
    )
    copies = [move.start(src, dst) for src, dst in pairs]
    rows = r.shape[0]
    wait(copies)
    inputs = r[...].astype(F32)
    upstream = g[...].astype(F32)
    gate = gate_ref[:, :1]
    attention = attn_own[...].astype(F32) + attn_other[...].astype(F32)
    branch = attention + (both_own[:rows].astype(F32) + both_other[:rows].astype(F32))
    out_ref[...] = (inputs + gate * branch).astype(BF)
    dl = jnp.sum(upstream * branch, axis=-1, keepdims=True) * gate * (1.0 - gate)
    d_router = jnp.sum(dl * inputs, axis=0, keepdims=True)
    dn1 = dn1_own[...].astype(F32) + dn1_other[...].astype(F32)
    inverse = lax.rsqrt(jnp.mean(inputs * inputs, axis=-1, keepdims=True) + epsilon)
    normal = inputs * inverse
    product = dn1 * normal
    d_gain = jnp.sum(product, axis=0, keepdims=True)
    gain = vec[0:1]
    dr = inverse * (dn1 * gain - normal * jnp.mean(product * gain, axis=-1, keepdims=True))
    back_ref[...] = (upstream + dh[...] + dl * vec[2:3] + dr).astype(BF)
    row = lax.broadcasted_iota(jnp.int32, (CAP, LANE), 0)
    total = jnp.zeros((1, LANE), F32)
    for s in range(rows // CAP):
        part = gate_ref[s * CAP : (s + 1) * CAP]
        total += jnp.sum(jnp.where(row < count_ref[s], part, 0.0), axis=0, keepdims=True)
    small_ref[0:1] = d_gain
    small_ref[1:2] = d_router
    small_ref[2:3] = jnp.concatenate([total] * (d_gain.shape[1] // LANE), axis=1)
    small_ref[3:8] = jnp.zeros((5, d_gain.shape[1]), F32)


def rows_last(counts, attn_own, attn_other, both_own, both_other, dn1_own, dn1_other, routed, upstream, gate, vec, dh):
    rows, width = routed.shape
    ins = (attn_own, attn_other, routed, upstream, gate, vec, dh)
    return call(
        rows_kernel,
        [sds((rows, width), BF), sds((rows, width), BF), sds((8, width), F32)], [VM] * 3,
        (counts, both_own, both_other, dn1_own, dn1_other, *ins), [SM] + [VM] * 4 + [ANY] * len(ins),
        [like(x.shape, x.dtype) for x in ins], len(ins), "rows_last", LIMITS[8],
    )


def body(
    tokens_in,
    route_mask,
    cotangent,
    w_query,
    w_key,
    w_value,
    w_out,
    w_up,
    w_down,
    gain_attn,
    gain_mlp,
    router,
):
    n = lax.axis_size("dp")
    mine, w = w_query.shape
    hidden = w_up.shape[1]
    width = tokens_in.shape[1]
    seqs = tokens_in.shape[0] // LEN
    extras = jnp.concatenate(
        [gain_attn[:, None], gain_mlp[:, None], router[:, None], jnp.zeros((mine, EXTRA - 3), BF)], axis=1
    )
    attn = Gather(jnp.concatenate([w_query, w_key, w_value, w_out.T, extras], axis=1), n)
    up = Gather(w_up, n)
    down = Gather(w_down.T, n)
    counts = jnp.sum(route_mask.reshape(seqs, LEN), axis=1).astype(jnp.int32)

    def start(chains, token, swaps=()):
        held = [c.held if isinstance(c, Gather) else c.send for c in chains]
        flat = tie([v for h in held for v in h] + list(swaps), token)
        arrived = []
        for chain, h in zip(chains, held):
            part, flat = flat[: len(h)], flat[len(h) :]
            if isinstance(chain, Gather):
                chain.held = part
            else:
                chain.send = part
            arrived += chain.begin()
        swapped = [other_core(v) for v in flat]
        return arrived + swapped, swapped

    def close(chains, made=()):
        flat = tie([g for c in chains for g in c.got], made)
        for chain in chains:
            chain.got, flat = flat[: len(chain.got)], flat[len(chain.got) :]
            chain.end()

    pos = places_of(width, n)
    four = attn.steps == 4

    token, _ = start([attn], [])
    routed, upstream, slot = pick(route_mask, tokens_in, cotangent, seqs)
    close([attn], [slot])
    for chains in ([attn, up], [attn, up], [attn, down]) if four else [[attn, up, down]] * (attn.steps - 1):
        token, _ = start(chains, token)
        close(chains)
    src_attn = attn.result()
    rest = [[up, down], [up, down], [down]] if four else [[up, down], [], []]
    token, _ = start(rest[0], token)
    n1, qkv, attended, attn_own, gate, vec, prob = attn_fwd(src_attn, counts, routed, w)
    close(rest[0], [attn_own])
    token, (attn_other,) = start(rest[1], token, [attn_own])
    close(rest[1])
    src_up = up.result()
    token, _ = start(rest[2], token)
    (h, n2, slope, z, dm), sum_down = mlp_up(
        src_up, pos, attn_own, attn_other, routed, upstream, gate, vec, hidden, n
    )
    close(rest[2], [dm])
    src_down = down.result()

    token, _ = start([sum_down], token)
    du, dn2_own = mlp_back(src_up, src_down, dm, slope)
    both_own = mlp_out(src_down, z, dn2_own)
    sum_up = grad_up(pos, n2, du, n)
    close([sum_down], sum_up.send + [both_own])
    token, (both_other,) = start([sum_up, sum_down], token, [both_own])
    (dh, dn1_own, gain_two), sum_attn = attn_back(
        src_attn, pos, both_own, both_other, h, vec, upstream, gate, qkv, prob, n1, attended, n
    )
    close([sum_up, sum_down], [gain_two])
    token, (dn1_other,) = start([sum_attn, sum_down], token, [dn1_own])
    down_there = token[-3:-1]
    close([sum_down])
    more, _ = start([sum_up], down_there)
    out_rows, back_rows, sums = rows_last(
        counts, attn_own, attn_other, both_own, both_other, dn1_own, dn1_other, routed, upstream, gate, vec, dh
    )
    block_out = place_rows(slot, tokens_in, out_rows, "place_out")
    close([sum_attn, sum_up], [block_out])
    token = token + more
    token, _ = start([sum_attn, sum_up, sum_down], token)
    (back_late,) = tie([back_rows], [token[3]])
    input_grad = place_rows(slot, cotangent, back_late, "place_grad")
    close([sum_attn, sum_up, sum_down], [input_grad])
    live = [c for c in (sum_attn, sum_up, sum_down) if c.at]
    first = True
    while live:
        token, _ = start(live, token)
        if first:
            first = False
            sums, gain_two = tie([sums, gain_two], [token[0]])
            scalars = jnp.stack([jnp.sum(counts).astype(F32), sums[2, 0]])
            small = jnp.concatenate(
                [
                    sums[0].reshape(n, mine),
                    gain_two[0].reshape(n, mine),
                    sums[1].reshape(n, mine),
                    jnp.broadcast_to(scalars, (n, 2)),
                ],
                axis=1,
            )
            small = lax.all_to_all(small, "dp", 0, 0, tiled=True)
        close(live)
        live = [c for c in live if c.at]
    small = jnp.sum(small, axis=0)
    total_attn, total_up, total_down = sum_attn.result(), sum_up.result(), sum_down.result()
    token_total = tokens_in.shape[0] * n
    return (
        block_out,
        input_grad,
        total_attn[:, :w],
        total_attn[:, w : 2 * w],
        total_attn[:, 2 * w : 3 * w],
        total_attn[:, 3 * w :].T,
        total_up,
        total_down.T,
        small[:mine],
        small[mine : 2 * mine],
        small[2 * mine : 3 * mine],
        small[3 * mine] / token_total,
        small[3 * mine + 1] / small[3 * mine],
    )


def solution(mesh):
    rows, cols = P("dp", "mp"), P("mp", "dp")
    return jax.shard_map(
        body,
        mesh=mesh,
        in_specs=(P("dp", None), P("dp"), P("dp", None), rows, rows, rows, cols, rows, cols) + (P("dp"),) * 3,
        out_specs=(P("dp", None), P("dp", None), rows, rows, rows, cols, rows, cols) + (P("dp"),) * 3 + (P(), P()),
        check_vma=False,
    )
```

```python
import jax
import jax.numpy as jnp
from jax import lax
from jax.experimental import pallas as pl
from jax.experimental.pallas import tpu as pltpu
from jax.sharding import PartitionSpec as P

HD = 64
LEN = 2048
CAP = 256
LANE = 128
EXTRA = 128
MIB = 1 << 20
LIMITS = (20, 28, 24, 12, 14, 34, 24, 46, 24)
FAR = 12
COST = pl.CostEstimate(flops=8000000000, bytes_accessed=24000000, transcendentals=0)

epsilon = 1e-06
negative = -1e30
BF = jnp.bfloat16
F32 = jnp.float32
SM = pl.BlockSpec(memory_space=pltpu.SMEM)
HB = pl.BlockSpec(memory_space=pltpu.HBM)
VM = pl.BlockSpec(memory_space=pltpu.VMEM)
ANY = pl.BlockSpec(memory_space=pl.ANY)


def nn(a, b):
    return jnp.dot(a, b, preferred_element_type=F32)


def nt(a, b):
    return lax.dot_general(a, b, (((1,), (1,)), ((), ())), preferred_element_type=F32)


def tn(a, b):
    return lax.dot_general(a, b, (((0,), (0,)), ((), ())), preferred_element_type=F32)


def sds(shape, dtype):
    return jax.ShapeDtypeStruct(shape, dtype)


def color_orders(n):
    bits = n.bit_length() - 1
    if bits == 4:
        x, y, z1, z2 = 1, 2, 4, 12
        return (((z2, y, z1, x), (z2, z1, x, y)), ((z2, x, y, z1), (z2, x, y, z1)))
    down = tuple(1 << b for b in reversed(range(bits)))
    return ((down, down), (down, down))


def bit_sum(n, index, source, target):
    total = jnp.zeros((n,), jnp.int32)
    for one, two in zip(source, target):
        total = total ^ jnp.where((index & one) != 0, two, 0)
    return total


def spots(orders):
    return [1 << k for k in range(len(orders[0]))]


def owners(n, orders):
    p = jnp.arange(n, dtype=jnp.int32)
    one, two = (bit_sum(n, p, spots(orders), o) for o in orders)
    return lax.axis_index("dp") ^ jnp.where(lax.axis_index("mp") == 0, one, two)


def places(n, orders):
    d = jnp.arange(n, dtype=jnp.int32) ^ lax.axis_index("dp")
    if any(12 in o for o in orders):
        d = d ^ ((d & 8) >> 1)
    plain = [[8 if bit == 12 else bit for bit in o] for o in orders]
    one, two = (bit_sum(n, d, o, spots(orders)) for o in plain)
    return jnp.where(lax.axis_index("mp") == 0, one, two)


def hop(array, n, one, two):
    pairs = [(d * 2 + c, (d ^ (one, two)[c]) * 2 + c) for d in range(n) for c in range(2)]
    return lax.ppermute(array, ("dp", "mp"), pairs)


def other_core(array):
    return lax.ppermute(array, "mp", [(0, 1), (1, 0)])


def split_of(width):
    return -(-width * 2 // (3 * LANE)) * LANE


class Gather:
    def __init__(self, shard, n):
        self.n = n
        self.orders = color_orders(n)
        self.steps = len(self.orders[0][0])
        self.at = 0
        self.width = shard.shape[1]
        self.cut = split_of(self.width)
        self.held = [shard]
        self.got = None

    def begin(self):
        k = self.at
        if k == 0:
            one, two = self.orders[0][0][0], self.orders[0][1][0]
            self.got = [hop(self.held[0], self.n, one, two)]
        else:
            self.got = [hop(h, self.n, o[0][k], o[1][k]) for h, o in zip(self.held, self.orders)]
        self.at += 1
        return self.got

    def end(self):
        if self.at == self.steps:
            return
        if self.at == 1:
            both = jnp.concatenate([self.held[0], self.got[0]], axis=0)
            self.held = [both[:, : self.cut], both[:, self.cut :]]
        else:
            self.held = [jnp.concatenate([h, g], axis=0) for h, g in zip(self.held, self.got)]

    def result(self):
        n = self.n
        ids = jnp.stack([owners(n, o) for o in self.orders])
        halves = [self.held[0], self.got[0], self.held[1], self.got[1]]
        rows = 2 * self.held[0].shape[0]
        if (rows // n) % 16:
            out = []
            for at, (h, g) in enumerate(zip(self.held, self.got)):
                blocks = jnp.concatenate([h, g], axis=0).reshape(n, rows // n, -1)
                blocks = blocks[places(n, self.orders[at])].reshape(rows, -1)
                out += [blocks[: rows // 2], blocks[rows // 2 :]]
            return jnp.zeros((2, 2), jnp.int32) + jnp.arange(2, dtype=jnp.int32), out
        return ids, halves


class Scatter:
    def __init__(self, keep, send, n):
        self.n = n
        self.orders = color_orders(n)
        self.steps = len(self.orders[0][0])
        self.at = self.steps
        self.keep, self.send = keep, send

    def ops(self):
        return self.send

    def begin(self):
        k = self.at - 1
        if len(self.send) == 1:
            one, two = self.orders[0][0][0], self.orders[0][1][0]
            self.got = [hop(self.send[0], self.n, one, two)]
        else:
            self.got = [hop(s, self.n, o[0][k], o[1][k]) for s, o in zip(self.send, self.orders)]
        self.at -= 1
        return self.got

    def end(self):
        half = self.got[0].shape[0] // 2
        if self.at == 0:
            self.keep = [k.astype(F32) + g.astype(F32) for k, g in zip(self.keep, self.got)]
            self.send = []
            return
        send = [(k[half:].astype(F32) + g[half:].astype(F32)).astype(BF) for k, g in zip(self.keep, self.got)]
        keep = [(k[:half].astype(F32) + g[:half].astype(F32)).astype(BF) for k, g in zip(self.keep, self.got)]
        if self.at == 1:
            keep = [jnp.concatenate(keep, axis=1)]
            send = [jnp.concatenate(send, axis=1)]
        self.keep, self.send = keep, send

    def result(self):
        return self.keep[0]


def tie(values, tokens):
    if not tokens:
        return list(values)
    out = lax.optimization_barrier(tuple(values) + tuple(tokens))
    return list(out[: len(values)])


def pick_kernel(mask_ref, x_ref, c_ref, r_ref, g_ref, slot_ref, sel):
    groups = mask_ref.shape[1]
    flag = mask_ref[0].astype(F32)
    up = lax.broadcasted_iota(jnp.int32, (LANE, LANE), 0) <= lax.broadcasted_iota(jnp.int32, (LANE, LANE), 1)
    within = nn(flag, up.astype(F32))
    total = jnp.broadcast_to(within[:, LANE - 1 :], (groups, LANE))
    low = lax.broadcasted_iota(jnp.int32, (groups, groups), 1) < lax.broadcasted_iota(
        jnp.int32, (groups, groups), 0
    )
    rank = within + nn(low.astype(F32), total) - 1.0
    slot = jnp.where(flag > 0, rank, -1.0)
    place = lax.broadcasted_iota(jnp.int32, (CAP, LANE), 0).astype(F32)
    for at in range(groups):
        slot_ref[at] = slot[at : at + 1]
        sel[:, at * LANE : (at + 1) * LANE] = jnp.where(place == slot[at : at + 1], 1.0, 0.0).astype(BF)
    r_ref[...] = nn(sel[...], x_ref[...]).astype(BF)
    g_ref[...] = nn(sel[...], c_ref[...]).astype(BF)


def pick(mask, tokens, cotangent, seqs):
    width = tokens.shape[1]
    groups = LEN // LANE
    return pl.pallas_call(
        pick_kernel,
        grid=(seqs,),
        in_specs=[
            pl.BlockSpec((1, groups, LANE), lambda s: (s, 0, 0)),
            pl.BlockSpec((LEN, width), lambda s: (s, 0)),
            pl.BlockSpec((LEN, width), lambda s: (s, 0)),
        ],
        out_specs=[
            pl.BlockSpec((CAP, width), lambda s: (s, 0)),
            pl.BlockSpec((CAP, width), lambda s: (s, 0)),
            pl.BlockSpec((groups, 1, LANE), lambda s: (s, 0, 0)),
        ],
        out_shape=[
            sds((seqs * CAP, width), BF),
            sds((seqs * CAP, width), BF),
            sds((seqs * groups, 1, LANE), F32),
        ],
        scratch_shapes=[pltpu.VMEM((CAP, LEN), BF)],
        compiler_params=pltpu.CompilerParams(vmem_limit_bytes=LIMITS[7] * MIB),
        cost_estimate=COST,
        name="pick",
    )(mask.reshape(seqs, groups, LANE), tokens, cotangent)


class Mover:
    def __init__(self, sem):
        self.sem = sem
        self.used = 0
        self.out = []

    def start(self, src, dst):
        copy = pltpu.make_async_copy(src, dst, self.sem.at[self.used])
        self.used += 1
        copy.start()
        return copy

    def put(self, src, dst):
        self.out.append(self.start(src, dst))

    def weights(self, ids_ref, halves, dst):
        blocks = ids_ref.shape[1]
        rows = dst.shape[0] // blocks
        copies = []
        col = 0
        for piece in range(2):
            width = halves[2 * piece].shape[1]
            for at in range(blocks):
                src = halves[2 * piece + at // (blocks // 2)]
                from_row = (at % (blocks // 2)) * rows
                to_row = pl.multiple_of(ids_ref[piece, at] * rows, rows)
                copies.append(
                    self.start(src.at[pl.ds(from_row, rows), :], dst.at[pl.ds(to_row, rows), pl.ds(col, width)])
                )
            col += width
        return copies

    def finish(self):
        wait(self.out)


def wait(copies):
    for copy in copies:
        copy.wait()


def like(shape, dtype=BF):
    return pltpu.VMEM(shape, dtype)


def call(kernel, out_shape, out_specs, args, in_specs, scratch, copies, name, limit):
    return pl.pallas_call(
        kernel,
        out_shape=out_shape,
        in_specs=in_specs,
        out_specs=out_specs,
        scratch_shapes=list(scratch) + [pltpu.SemaphoreType.DMA((copies,))],
        compiler_params=pltpu.CompilerParams(vmem_limit_bytes=limit * MIB),
        cost_estimate=COST,
        name=name,
    )(*args)


def softmax(queries, keys, allowed):
    scores = nt(queries, keys) * (HD**-0.5)
    scores = jnp.where(allowed, scores, negative)
    raised = jnp.exp(scores - jnp.max(scores, axis=-1, keepdims=True))
    return raised / jnp.sum(raised, axis=-1, keepdims=True)


def allowed_slots(count):
    row = lax.broadcasted_iota(jnp.int32, (CAP, CAP), 0)
    col = lax.broadcasted_iota(jnp.int32, (CAP, CAP), 1)
    return (col <= row) & (col < count)


def attn_fwd_kernel(
    ids, count_ref, r, s0, s1, s2, s3, n1, qkv, o, part, gate, vec, p_hbm, weights, prob, sem
):
    move = Mover(sem)
    copies = move.weights(ids, (s0, s1, s2, s3), weights)
    w = o.shape[1]
    seqs = r.shape[0] // CAP
    inputs = r[...].astype(F32)
    normal = inputs * lax.rsqrt(jnp.mean(inputs * inputs, axis=-1, keepdims=True) + epsilon)
    wait(copies)
    vectors = weights[:, 4 * w :].astype(F32).T[:8]
    vec[...] = vectors
    n1[...] = (normal * vectors[0:1]).astype(BF)
    logit = jnp.sum(inputs * vectors[2:3], axis=-1, keepdims=True)
    gate[...] = jnp.broadcast_to(jax.nn.sigmoid(logit), gate.shape)
    qkv[...] = nn(n1[...], weights[:, : 3 * w]).astype(BF)
    first = lax.broadcasted_iota(jnp.int32, (CAP, 2 * HD), 1) < HD
    pairs = w // (2 * HD)
    for s in range(seqs):
        allowed = allowed_slots(count_ref[s])
        rows = slice(s * CAP, (s + 1) * CAP)
        for pair in range(pairs):
            at = pair * 2 * HD
            q = qkv[rows, at : at + 2 * HD]
            k = qkv[rows, w + at : w + at + 2 * HD]
            v = qkv[rows, 2 * w + at : 2 * w + at + 2 * HD]
            zero = jnp.zeros_like(q)
            one = softmax(jnp.where(first, q, zero), k, allowed)
            two = softmax(jnp.where(first, zero, q), k, allowed)
            head = 2 * (s * pairs + pair)
            prob[head] = one
            prob[head + 1] = two
            o[rows, at : at + 2 * HD] = jnp.where(first, nn(one.astype(BF), v), nn(two.astype(BF), v)).astype(BF)
        half = pl.ds(2 * s * pairs, 2 * pairs)
        move.put(prob.at[half], p_hbm.at[half])
    part[...] = nt(o[...], weights[:, 3 * w : 4 * w]).astype(BF)
    move.finish()


def attn_fwd(source, counts, routed, w):
    ids, halves = source
    rows, width = routed.shape
    heads = rows // CAP * w // HD
    outs = [
        sds((rows, width), BF), sds((rows, 3 * w), BF), sds((rows, w), BF), sds((rows, width), BF),
        sds((rows, LANE), F32), sds((8, width), F32), sds((FAR * heads, CAP, CAP), F32),
    ]
    return call(
        attn_fwd_kernel, outs, [VM] * 6 + [HB],
        (ids, counts, routed, *halves), [SM, SM, VM] + [ANY] * 4,
        [like((width, 4 * w + EXTRA)), like((heads, CAP, CAP), F32)],
        2 * ids.shape[1] + 4, "attn_fwd", LIMITS[0],
    )


def grad_into(pos, lefts, rights, outs):
    blocks = pos.shape[1]
    width = 2 * outs[0].shape[0]
    rows = width // blocks
    tile = 256
    for at in range(0, width, tile):
        for piece in range(2):
            keep, send = outs[2 * piece], outs[2 * piece + 1]
            col = 0
            for left, right in zip(lefts[piece], rights[piece]):
                value = tn(left[:, at : at + tile], right).astype(BF)
                cols = slice(col, col + right.shape[1])
                col += right.shape[1]
                for b in range(0, tile, rows):
                    place = pos[piece, (at + b) // rows]
                    block = value[b : b + rows]

                    @pl.when(place < blocks // 2)
                    def _():
                        keep[pl.ds(pl.multiple_of(place * rows, rows), rows), cols] = block

                    @pl.when(place >= blocks // 2)
                    def _():
                        send[pl.ds(pl.multiple_of((place - blocks // 2) * rows, rows), rows), cols] = block


def mlp_up_kernel(
    ids, pos, own, other, r, vec, gate, g, s0, s1, s2, s3,
    h_hbm, n2, slope_hbm, z_hbm, dm, k0, d0, k1, d1, h, slope, z, weights, sem,
):
    move = Mover(sem)
    copies = move.weights(ids, (s0, s1, s2, s3), weights)
    h[...] = r[...].astype(F32) + (own[...].astype(F32) + other[...].astype(F32))
    move.put(h, h_hbm)
    normal = h[...] * lax.rsqrt(jnp.mean(h[...] * h[...], axis=-1, keepdims=True) + epsilon)
    n2[...] = (normal * vec[1:2]).astype(BF)
    dm[...] = (gate[:, :1] * g[...].astype(F32)).astype(BF)
    wait(copies)
    a, c = 0.044715, 0.7978845608028654
    step = 512
    for at in range(0, weights.shape[1], step):
        cols = slice(at, at + step)
        u = nn(n2[...], weights[:, cols])
        square = u * u
        t = jnp.tanh(c * (u + a * (square * u)))
        half = 0.5 * (1.0 + t)
        z[:, cols] = (u * half).astype(BF)
        slope[:, cols] = half + 0.5 * u * (1.0 - t * t) * (c * (1.0 + 3.0 * a * square))
        move.put(slope.at[:, pl.ds(at, step)], slope_hbm.at[pl.ds(0, slope.shape[0]), pl.ds(at, step)])
    move.put(z, z_hbm)
    cut = k0.shape[1]
    grad_into(pos, [[dm], [dm]], [[z[:, :cut]], [z[:, cut:]]], (k0, d0, k1, d1))
    move.finish()


def places_of(width, n):
    if (width // n) % 16 == 0:
        return jnp.stack([places(n, o) for o in color_orders(n)])
    return jnp.zeros((2, 16), jnp.int32) + jnp.arange(16, dtype=jnp.int32)


def grad_shapes(width, total):
    cut = split_of(total)
    return [sds((width // 2, c), BF) for c in (cut, cut, total - cut, total - cut)]


def scatter_of(outs, width, n):
    keep0, send0, keep1, send1 = outs
    keep, send = [keep0, keep1], [send0, send1]
    if (width // n) % 16:
        orders = color_orders(n)
        for at in range(2):
            whole = jnp.concatenate([keep[at], send[at]], axis=0).reshape(n, width // n, -1)
            whole = whole[owners(n, orders[at])].reshape(width, -1)
            keep[at], send[at] = whole[: width // 2], whole[width // 2 :]
    return Scatter(keep, send, n)


def mlp_up(source, pos, own, other, routed, upstream, gate, vec, hidden, n):
    ids, halves = source
    rows, width = routed.shape
    outs = [
        sds((rows, width), F32), sds((rows, width), BF), sds((FAR * rows, hidden), F32),
        sds((rows, hidden), BF), sds((rows, width), BF),
    ]
    result = call(
        mlp_up_kernel, outs + grad_shapes(width, hidden), [HB, VM, HB, HB, VM] + [VM] * 4,
        (ids, pos, own, other, routed, vec, gate, upstream, *halves), [SM] * 2 + [VM] * 6 + [ANY] * 4,
        [like((rows, width), F32), like((rows, hidden), F32), like((rows, hidden)), like((width, hidden))],
        2 * ids.shape[1] + 16, "mlp_up", LIMITS[1],
    )
    return result[:5], scatter_of(result[5:], width, n)


def mlp_back_kernel(
    idu, idd, dm, slope_hbm, u0, u1, u2, u3, d0, d1, d2, d3, du, part, slope, wu, wd, sem
):
    move = Mover(sem)
    step = 512
    down = move.weights(idd, (d0, d1, d2, d3), wd)
    tiles = [
        move.start(slope_hbm.at[pl.ds(0, slope.shape[0]), pl.ds(at, step)], slope.at[:, pl.ds(at, step)])
        for at in range(0, wd.shape[1], step)
    ]
    up = move.weights(idu, (u0, u1, u2, u3), wu)
    wait(down)
    for at in range(0, wd.shape[1], step):
        dz = nn(dm[...], wd[:, at : at + step])
        tiles[at // step].wait()
        du[:, at : at + step] = (dz * slope[:, at : at + step]).astype(BF)
    wait(up)
    part[...] = nt(du[...], wu[...]).astype(BF)


def mlp_back(up, down, dm, slope):
    rows, width = dm.shape
    hidden = slope.shape[1]
    return call(
        mlp_back_kernel, [sds((rows, hidden), BF), sds((rows, width), BF)], [VM, VM],
        (up[0], down[0], dm, slope, *up[1], *down[1]), [SM, SM, VM, HB] + [ANY] * 8,
        [like((rows, hidden), F32)] + [like((width, hidden))] * 2,
        4 * up[0].shape[1] + 8, "mlp_back", LIMITS[2],
    )


def grad_up_kernel(pos, n2, du, k0, d0, k1, d1, sem):
    cut = k0.shape[1]
    grad_into(pos, [[n2], [n2]], [[du[:, :cut]], [du[:, cut:]]], (k0, d0, k1, d1))


def grad_up(pos, n2, du, n):
    width = n2.shape[1]
    hidden = du.shape[1]
    result = call(
        grad_up_kernel, grad_shapes(width, hidden), [VM] * 4,
        (pos, n2, du), [SM, VM, VM], [], 1, "grad_up", LIMITS[3],
    )
    return scatter_of(result, width, n)


def mlp_out_kernel(idd, dn1, z_hbm, d0, d1, d2, d3, both, z, wd, sem):
    move = Mover(sem)
    first = move.start(z_hbm, z)
    copies = move.weights(idd, (d0, d1, d2, d3), wd)
    rows = dn1.shape[0]
    both[rows:] = dn1[...]
    wait(copies)
    first.wait()
    both[:rows] = nt(z[...], wd[...]).astype(BF)


def mlp_out(down, z, dn1):
    rows, hidden = z.shape
    width = dn1.shape[1]
    return call(
        mlp_out_kernel, sds((2 * rows, width), BF), VM,
        (down[0], dn1, z, *down[1]), [SM, VM, HB] + [ANY] * 4,
        [like((rows, hidden)), like((width, hidden))],
        2 * down[0].shape[1] + 8, "mlp_out", LIMITS[4],
    )


def attn_back_kernel(
    ids, pos, own, other, vec, gate, g, qkv, n1, o, h_hbm, p_hbm, s0, s1, s2, s3,
    dh_hbm, part, gain_out, k0, d0, k1, d1, h, prob, dh, weights, da, do_ref, dqkv, sem,
):
    move = Mover(sem)
    early = move.start(h_hbm, h)
    copies = move.weights(ids, (s0, s1, s2, s3), weights)
    heads_in = move.start(p_hbm.at[pl.ds(0, prob.shape[0])], prob)
    rows = h.shape[0]
    w = do_ref.shape[1]
    dn2 = own[rows:].astype(F32) + other[rows:].astype(F32)
    early.wait()
    inverse = lax.rsqrt(jnp.mean(h[...] * h[...], axis=-1, keepdims=True) + epsilon)
    normal = h[...] * inverse
    product = dn2 * normal
    gain_out[...] = jnp.broadcast_to(jnp.sum(product, axis=0, keepdims=True), gain_out.shape)
    gain = vec[1:2]
    dh[...] = inverse * (dn2 * gain - normal * jnp.mean(product * gain, axis=-1, keepdims=True))
    move.put(dh, dh_hbm)
    da[...] = (gate[:, :1] * g[...].astype(F32) + dh[...]).astype(BF)
    wait(copies)
    do_ref[...] = nn(da[...], weights[:, 3 * w : 4 * w]).astype(BF)
    heads_in.wait()
    first = lax.broadcasted_iota(jnp.int32, (CAP, 2 * HD), 1) < HD
    scale = HD**-0.5
    pairs = w // (2 * HD)
    for s in range(rows // CAP):
        at_rows = slice(s * CAP, (s + 1) * CAP)
        for pair in range(pairs):
            at = pair * 2 * HD
            q = qkv[at_rows, at : at + 2 * HD]
            k = qkv[at_rows, w + at : w + at + 2 * HD]
            v = qkv[at_rows, 2 * w + at : 2 * w + at + 2 * HD]
            do = do_ref[at_rows, at : at + 2 * HD]
            zero = jnp.zeros_like(q)
            results = []
            for head in range(2):
                do_one = jnp.where(first, do, zero) if head == 0 else jnp.where(first, zero, do)
                probability = prob[2 * (s * pairs + pair) + head]
                d_probability = nt(do_one, v)
                dv = tn(probability.astype(BF), do)
                inner = jnp.sum(probability * d_probability, axis=-1, keepdims=True)
                ds = (probability * (d_probability - inner)).astype(BF)
                results.append((nn(ds, k) * scale, tn(ds, q) * scale, dv))
            for which in range(3):
                value = jnp.where(first, results[0][which], results[1][which]).astype(BF)
                dqkv[at_rows, which * w + at : which * w + at + 2 * HD] = value
    cut = k0.shape[1]
    grad_into(pos, [[n1], [n1, da]], [[dqkv[:, :cut]], [dqkv[:, cut:], o[...]]], (k0, d0, k1, d1))
    part[...] = nt(dqkv[...], weights[:, : 3 * w]).astype(BF)
    move.finish()


def attn_back(source, pos, own, other, h, vec, upstream, gate, qkv, prob, n1, attended, n):
    ids, halves = source
    rows, width = h.shape
    w = attended.shape[1]
    outs = [sds((rows, width), F32), sds((rows, width), BF), sds((8, width), F32)]
    result = call(
        attn_back_kernel, outs + grad_shapes(width, 4 * w), [HB, VM, VM] + [VM] * 4,
        (ids, pos, own, other, vec, gate, upstream, qkv, n1, attended, h, prob, *halves),
        [SM] * 2 + [VM] * 8 + [HB] * 2 + [ANY] * 4,
        [
            like((rows, width), F32), like((prob.shape[0] // FAR, CAP, CAP), F32), like((rows, width), F32),
            like((width, 4 * w + EXTRA)), like((rows, width)), like((rows, w)), like((rows, 3 * w)),
        ],
        2 * ids.shape[1] + 8, "attn_back", LIMITS[5],
    )
    return result[:3], scatter_of(result[3:], width, n)


TILE = 1024


def select_rows(slot_ref, sel, rows, x_ref, out_ref):
    place = lax.broadcasted_iota(jnp.int32, (CAP, LANE), 0).astype(F32)
    for at in range(TILE // LANE):
        sel[:, at * LANE : (at + 1) * LANE] = jnp.where(place == slot_ref[at], 1.0, 0.0).astype(BF)
    put = tn(sel[...], rows[...])
    hit = tn(sel[...], jnp.ones((CAP, LANE), BF))[:, :1]
    out_ref[...] = jnp.where(hit > 0.5, put.astype(BF), x_ref[...])


def place_kernel(slot_ref, x_ref, rows, out_ref, sel):
    select_rows(slot_ref, sel, rows, x_ref, out_ref)


def place_rows(slot, tokens, rows, name):
    width = tokens.shape[1]
    per = LEN // TILE
    seqs = tokens.shape[0] // LEN
    groups = TILE // LANE
    return pl.pallas_call(
        place_kernel,
        grid=(seqs, per),
        in_specs=[
            pl.BlockSpec((groups, 1, LANE), lambda s, t: (s * per + t, 0, 0)),
            pl.BlockSpec((TILE, width), lambda s, t: (s * per + t, 0)),
            pl.BlockSpec((CAP, width), lambda s, t: (s, 0)),
        ],
        out_specs=pl.BlockSpec((TILE, width), lambda s, t: (s * per + t, 0)),
        out_shape=sds(tokens.shape, BF),
        scratch_shapes=[pltpu.VMEM((CAP, TILE), BF)],
        compiler_params=pltpu.CompilerParams(vmem_limit_bytes=LIMITS[6] * MIB),
        cost_estimate=COST,
        name=name,
    )(slot, tokens, rows)


def rows_kernel(
    count_ref, both_own, both_other, dn1_own, dn1_other, attn_own_any, attn_other_any, r_any, g_any, gate_any, vec_any, dh_any,
    out_ref, back_ref, small_ref, attn_own, attn_other, r, g, gate_ref, vec, dh, sem,
):
    move = Mover(sem)
    pairs = (
        (r_any, r), (g_any, g), (attn_own_any, attn_own), (attn_other_any, attn_other),
        (gate_any, gate_ref), (vec_any, vec), (dh_any, dh),
    )
    copies = [move.start(src, dst) for src, dst in pairs]
    rows = r.shape[0]
    wait(copies)
    inputs = r[...].astype(F32)
    upstream = g[...].astype(F32)
    gate = gate_ref[:, :1]
    attention = attn_own[...].astype(F32) + attn_other[...].astype(F32)
    branch = attention + (both_own[:rows].astype(F32) + both_other[:rows].astype(F32))
    out_ref[...] = (inputs + gate * branch).astype(BF)
    dl = jnp.sum(upstream * branch, axis=-1, keepdims=True) * gate * (1.0 - gate)
    d_router = jnp.sum(dl * inputs, axis=0, keepdims=True)
    dn1 = dn1_own[...].astype(F32) + dn1_other[...].astype(F32)
    inverse = lax.rsqrt(jnp.mean(inputs * inputs, axis=-1, keepdims=True) + epsilon)
    normal = inputs * inverse
    product = dn1 * normal
    d_gain = jnp.sum(product, axis=0, keepdims=True)
    gain = vec[0:1]
    dr = inverse * (dn1 * gain - normal * jnp.mean(product * gain, axis=-1, keepdims=True))
    back_ref[...] = (upstream + dh[...] + dl * vec[2:3] + dr).astype(BF)
    row = lax.broadcasted_iota(jnp.int32, (CAP, LANE), 0)
    total = jnp.zeros((1, LANE), F32)
    for s in range(rows // CAP):
        part = gate_ref[s * CAP : (s + 1) * CAP]
        total += jnp.sum(jnp.where(row < count_ref[s], part, 0.0), axis=0, keepdims=True)
    small_ref[0:1] = d_gain
    small_ref[1:2] = d_router
    small_ref[2:3] = jnp.concatenate([total] * (d_gain.shape[1] // LANE), axis=1)
    small_ref[3:8] = jnp.zeros((5, d_gain.shape[1]), F32)


def rows_last(counts, attn_own, attn_other, both_own, both_other, dn1_own, dn1_other, routed, upstream, gate, vec, dh):
    rows, width = routed.shape
    ins = (attn_own, attn_other, routed, upstream, gate, vec, dh)
    return call(
        rows_kernel,
        [sds((rows, width), BF), sds((rows, width), BF), sds((8, width), F32)], [VM] * 3,
        (counts, both_own, both_other, dn1_own, dn1_other, *ins), [SM] + [VM] * 4 + [ANY] * len(ins),
        [like(x.shape, x.dtype) for x in ins], len(ins), "rows_last", LIMITS[8],
    )


def body(
    tokens_in,
    route_mask,
    cotangent,
    w_query,
    w_key,
    w_value,
    w_out,
    w_up,
    w_down,
    gain_attn,
    gain_mlp,
    router,
):
    n = lax.axis_size("dp")
    mine, w = w_query.shape
    hidden = w_up.shape[1]
    width = tokens_in.shape[1]
    seqs = tokens_in.shape[0] // LEN
    extras = jnp.concatenate(
        [gain_attn[:, None], gain_mlp[:, None], router[:, None], jnp.zeros((mine, EXTRA - 3), BF)], axis=1
    )
    attn = Gather(jnp.concatenate([w_query, w_key, w_value, w_out.T, extras], axis=1), n)
    up = Gather(w_up, n)
    down = Gather(w_down.T, n)
    counts = jnp.sum(route_mask.reshape(seqs, LEN), axis=1).astype(jnp.int32)

    def start(chains, token, swaps=()):
        held = [c.held if isinstance(c, Gather) else c.send for c in chains]
        flat = tie([v for h in held for v in h] + list(swaps), token)
        arrived = []
        for chain, h in zip(chains, held):
            part, flat = flat[: len(h)], flat[len(h) :]
            if isinstance(chain, Gather):
                chain.held = part
            else:
                chain.send = part
            arrived += chain.begin()
        swapped = [other_core(v) for v in flat]
        return arrived + swapped, swapped

    def close(chains, made=()):
        flat = tie([g for c in chains for g in c.got], made)
        for chain in chains:
            chain.got, flat = flat[: len(chain.got)], flat[len(chain.got) :]
            chain.end()

    pos = places_of(width, n)
    four = attn.steps == 4

    token, _ = start([attn], [])
    routed, upstream, slot = pick(route_mask, tokens_in, cotangent, seqs)
    close([attn], [slot])
    for chains in ([attn, up], [attn, up], [attn, down]) if four else [[attn, up, down]] * (attn.steps - 1):
        token, _ = start(chains, token)
        close(chains)
    src_attn = attn.result()
    rest = [[up, down], [up, down], [down]] if four else [[up, down], [], []]
    token, _ = start(rest[0], token)
    n1, qkv, attended, attn_own, gate, vec, prob = attn_fwd(src_attn, counts, routed, w)
    close(rest[0], [attn_own])
    token, (attn_other,) = start(rest[1], token, [attn_own])
    close(rest[1])
    src_up = up.result()
    token, _ = start(rest[2], token)
    (h, n2, slope, z, dm), sum_down = mlp_up(
        src_up, pos, attn_own, attn_other, routed, upstream, gate, vec, hidden, n
    )
    close(rest[2], [dm])
    src_down = down.result()

    token, _ = start([sum_down], token)
    du, dn2_own = mlp_back(src_up, src_down, dm, slope)
    both_own = mlp_out(src_down, z, dn2_own)
    sum_up = grad_up(pos, n2, du, n)
    close([sum_down], sum_up.send + [both_own])
    token, (both_other,) = start([sum_up, sum_down], token, [both_own])
    (dh, dn1_own, gain_two), sum_attn = attn_back(
        src_attn, pos, both_own, both_other, h, vec, upstream, gate, qkv, prob, n1, attended, n
    )
    close([sum_up, sum_down], [gain_two])
    token, (dn1_other,) = start([sum_attn, sum_down], token, [dn1_own])
    down_there = token[-3:-1]
    close([sum_down])
    more, _ = start([sum_up], down_there)
    out_rows, back_rows, sums = rows_last(
        counts, attn_own, attn_other, both_own, both_other, dn1_own, dn1_other, routed, upstream, gate, vec, dh
    )
    block_out = place_rows(slot, tokens_in, out_rows, "place_out")
    close([sum_attn, sum_up], [block_out])
    token = token + more
    token, _ = start([sum_attn, sum_up, sum_down], token)
    (back_late,) = tie([back_rows], [token[3]])
    input_grad = place_rows(slot, cotangent, back_late, "place_grad")
    close([sum_attn, sum_up, sum_down], [input_grad])
    live = [c for c in (sum_attn, sum_up, sum_down) if c.at]
    first = True
    while live:
        token, _ = start(live, token)
        if first:
            first = False
            sums, gain_two = tie([sums, gain_two], [token[0]])
            scalars = jnp.where(jnp.arange(width) % mine == 0, jnp.sum(counts).astype(F32), sums[2])
            small = jnp.stack([sums[0], gain_two[0], sums[1], scalars])
            small = small.reshape(4, n, mine).transpose(1, 0, 2).reshape(n, 4 * mine)
            small = lax.all_to_all(small, "dp", 0, 0, tiled=True)
        close(live)
        live = [c for c in live if c.at]
    small = jnp.sum(small, axis=0)
    total_attn, total_up, total_down = sum_attn.result(), sum_up.result(), sum_down.result()
    token_total = tokens_in.shape[0] * n
    return (
        block_out,
        input_grad,
        total_attn[:, :w],
        total_attn[:, w : 2 * w],
        total_attn[:, 2 * w : 3 * w],
        total_attn[:, 3 * w :].T,
        total_up,
        total_down.T,
        small[:mine],
        small[mine : 2 * mine],
        small[2 * mine : 3 * mine],
        small[3 * mine] / token_total,
        small[3 * mine + 1] / small[3 * mine],
    )


def solution(mesh):
    rows, cols = P("dp", "mp"), P("mp", "dp")
    return jax.shard_map(
        body,
        mesh=mesh,
        in_specs=(P("dp", None), P("dp"), P("dp", None), rows, rows, rows, cols, rows, cols) + (P("dp"),) * 3,
        out_specs=(P("dp", None), P("dp", None), rows, rows, rows, cols, rows, cols) + (P("dp"),) * 3 + (P(), P()),
        check_vma=False,
    )
```

```python
import jax
import jax.numpy as jnp
from jax import lax
from jax.experimental import pallas as pl
from jax.experimental.pallas import tpu as pltpu
from jax.sharding import PartitionSpec as P

HD = 64
LEN = 2048
CAP = 256
LANE = 128
EXTRA = 128
MIB = 1 << 20
LIMITS = (20, 28, 24, 12, 14, 34, 24, 46, 24)
FAR = 12
COST = pl.CostEstimate(flops=8000000000, bytes_accessed=24000000, transcendentals=0)

epsilon = 1e-06
negative = -1e30
BF = jnp.bfloat16
F32 = jnp.float32
SM = pl.BlockSpec(memory_space=pltpu.SMEM)
HB = pl.BlockSpec(memory_space=pltpu.HBM)
VM = pl.BlockSpec(memory_space=pltpu.VMEM)
ANY = pl.BlockSpec(memory_space=pl.ANY)


def nn(a, b):
    return jnp.dot(a, b, preferred_element_type=F32)


def nt(a, b):
    return lax.dot_general(a, b, (((1,), (1,)), ((), ())), preferred_element_type=F32)


def tn(a, b):
    return lax.dot_general(a, b, (((0,), (0,)), ((), ())), preferred_element_type=F32)


def sds(shape, dtype):
    return jax.ShapeDtypeStruct(shape, dtype)


def color_orders(n):
    bits = n.bit_length() - 1
    if bits == 4:
        x, y, z1, z2 = 1, 2, 4, 12
        return (((z2, y, z1, x), (z2, z1, x, y)), ((z2, x, y, z1), (z2, x, y, z1)))
    down = tuple(1 << b for b in reversed(range(bits)))
    return ((down, down), (down, down))


def bit_sum(n, index, source, target):
    total = jnp.zeros((n,), jnp.int32)
    for one, two in zip(source, target):
        total = total ^ jnp.where((index & one) != 0, two, 0)
    return total


def spots(orders):
    return [1 << k for k in range(len(orders[0]))]


def owners(n, orders):
    p = jnp.arange(n, dtype=jnp.int32)
    one, two = (bit_sum(n, p, spots(orders), o) for o in orders)
    return lax.axis_index("dp") ^ jnp.where(lax.axis_index("mp") == 0, one, two)


def places(n, orders):
    d = jnp.arange(n, dtype=jnp.int32) ^ lax.axis_index("dp")
    if any(12 in o for o in orders):
        d = d ^ ((d & 8) >> 1)
    plain = [[8 if bit == 12 else bit for bit in o] for o in orders]
    one, two = (bit_sum(n, d, o, spots(orders)) for o in plain)
    return jnp.where(lax.axis_index("mp") == 0, one, two)


def hop(array, n, one, two):
    pairs = [(d * 2 + c, (d ^ (one, two)[c]) * 2 + c) for d in range(n) for c in range(2)]
    return lax.ppermute(array, ("dp", "mp"), pairs)


def other_core(array):
    return lax.ppermute(array, "mp", [(0, 1), (1, 0)])


def split_of(width):
    return -(-width * 2 // (3 * LANE)) * LANE


class Gather:
    def __init__(self, shard, n):
        self.n = n
        self.orders = color_orders(n)
        self.steps = len(self.orders[0][0])
        self.at = 0
        self.width = shard.shape[1]
        self.cut = split_of(self.width)
        self.held = [shard]
        self.got = None

    def begin(self):
        k = self.at
        if k == 0:
            one, two = self.orders[0][0][0], self.orders[0][1][0]
            self.got = [hop(self.held[0], self.n, one, two)]
        else:
            self.got = [hop(h, self.n, o[0][k], o[1][k]) for h, o in zip(self.held, self.orders)]
        self.at += 1
        return self.got

    def end(self):
        if self.at == self.steps:
            return
        if self.at == 1:
            both = jnp.concatenate([self.held[0], self.got[0]], axis=0)
            self.held = [both[:, : self.cut], both[:, self.cut :]]
        else:
            self.held = [jnp.concatenate([h, g], axis=0) for h, g in zip(self.held, self.got)]

    def result(self):
        n = self.n
        ids = jnp.stack([owners(n, o) for o in self.orders])
        halves = [self.held[0], self.got[0], self.held[1], self.got[1]]
        rows = 2 * self.held[0].shape[0]
        if (rows // n) % 16:
            out = []
            for at, (h, g) in enumerate(zip(self.held, self.got)):
                blocks = jnp.concatenate([h, g], axis=0).reshape(n, rows // n, -1)
                blocks = blocks[places(n, self.orders[at])].reshape(rows, -1)
                out += [blocks[: rows // 2], blocks[rows // 2 :]]
            return jnp.zeros((2, 2), jnp.int32) + jnp.arange(2, dtype=jnp.int32), out
        return ids, halves


class Scatter:
    def __init__(self, keep, send, n, apart=False):
        self.n = n
        self.orders = color_orders(n)
        self.steps = len(self.orders[0][0])
        self.at = self.steps
        self.keep, self.send = keep, send
        self.apart = apart

    def ops(self):
        return self.send

    def begin(self):
        k = self.at - 1
        if len(self.send) == 1:
            one, two = self.orders[0][0][0], self.orders[0][1][0]
            self.got = [hop(self.send[0], self.n, one, two)]
        else:
            self.got = [hop(s, self.n, o[0][k], o[1][k]) for s, o in zip(self.send, self.orders)]
        self.at -= 1
        return self.got

    def end(self):
        half = self.got[0].shape[0] // 2
        if self.at == 0:
            self.keep = [k.astype(F32) + g.astype(F32) for k, g in zip(self.keep, self.got)]
            self.send = []
            return
        send = [(k[half:].astype(F32) + g[half:].astype(F32)).astype(BF) for k, g in zip(self.keep, self.got)]
        keep = [(k[:half].astype(F32) + g[:half].astype(F32)).astype(BF) for k, g in zip(self.keep, self.got)]
        if self.at == 1 and not self.apart:
            keep = [jnp.concatenate(keep, axis=1)]
            send = [jnp.concatenate(send, axis=1)]
        self.keep, self.send = keep, send

    def result(self):
        return jnp.concatenate(self.keep, axis=1) if len(self.keep) > 1 else self.keep[0]


def tie(values, tokens):
    if not tokens:
        return list(values)
    out = lax.optimization_barrier(tuple(values) + tuple(tokens))
    return list(out[: len(values)])


def pick_kernel(mask_ref, x_ref, c_ref, r_ref, g_ref, slot_ref, sel):
    groups = mask_ref.shape[1]
    flag = mask_ref[0].astype(F32)
    up = lax.broadcasted_iota(jnp.int32, (LANE, LANE), 0) <= lax.broadcasted_iota(jnp.int32, (LANE, LANE), 1)
    within = nn(flag, up.astype(F32))
    total = jnp.broadcast_to(within[:, LANE - 1 :], (groups, LANE))
    low = lax.broadcasted_iota(jnp.int32, (groups, groups), 1) < lax.broadcasted_iota(
        jnp.int32, (groups, groups), 0
    )
    rank = within + nn(low.astype(F32), total) - 1.0
    slot = jnp.where(flag > 0, rank, -1.0)
    place = lax.broadcasted_iota(jnp.int32, (CAP, LANE), 0).astype(F32)
    for at in range(groups):
        slot_ref[at] = slot[at : at + 1]
        sel[:, at * LANE : (at + 1) * LANE] = jnp.where(place == slot[at : at + 1], 1.0, 0.0).astype(BF)
    r_ref[...] = nn(sel[...], x_ref[...]).astype(BF)
    g_ref[...] = nn(sel[...], c_ref[...]).astype(BF)


def pick(mask, tokens, cotangent, seqs):
    width = tokens.shape[1]
    groups = LEN // LANE
    return pl.pallas_call(
        pick_kernel,
        grid=(seqs,),
        in_specs=[
            pl.BlockSpec((1, groups, LANE), lambda s: (s, 0, 0)),
            pl.BlockSpec((LEN, width), lambda s: (s, 0)),
            pl.BlockSpec((LEN, width), lambda s: (s, 0)),
        ],
        out_specs=[
            pl.BlockSpec((CAP, width), lambda s: (s, 0)),
            pl.BlockSpec((CAP, width), lambda s: (s, 0)),
            pl.BlockSpec((groups, 1, LANE), lambda s: (s, 0, 0)),
        ],
        out_shape=[
            sds((seqs * CAP, width), BF),
            sds((seqs * CAP, width), BF),
            sds((seqs * groups, 1, LANE), F32),
        ],
        scratch_shapes=[pltpu.VMEM((CAP, LEN), BF)],
        compiler_params=pltpu.CompilerParams(vmem_limit_bytes=LIMITS[7] * MIB),
        cost_estimate=COST,
        name="pick",
    )(mask.reshape(seqs, groups, LANE), tokens, cotangent)


class Mover:
    def __init__(self, sem):
        self.sem = sem
        self.used = 0
        self.out = []

    def start(self, src, dst):
        copy = pltpu.make_async_copy(src, dst, self.sem.at[self.used])
        self.used += 1
        copy.start()
        return copy

    def put(self, src, dst):
        self.out.append(self.start(src, dst))

    def weights(self, ids_ref, halves, dst):
        blocks = ids_ref.shape[1]
        rows = dst.shape[0] // blocks
        copies = []
        col = 0
        for piece in range(2):
            width = halves[2 * piece].shape[1]
            for at in range(blocks):
                src = halves[2 * piece + at // (blocks // 2)]
                from_row = (at % (blocks // 2)) * rows
                to_row = pl.multiple_of(ids_ref[piece, at] * rows, rows)
                copies.append(
                    self.start(src.at[pl.ds(from_row, rows), :], dst.at[pl.ds(to_row, rows), pl.ds(col, width)])
                )
            col += width
        return copies

    def finish(self):
        wait(self.out)


def wait(copies):
    for copy in copies:
        copy.wait()


def like(shape, dtype=BF):
    return pltpu.VMEM(shape, dtype)


def call(kernel, out_shape, out_specs, args, in_specs, scratch, copies, name, limit):
    return pl.pallas_call(
        kernel,
        out_shape=out_shape,
        in_specs=in_specs,
        out_specs=out_specs,
        scratch_shapes=list(scratch) + [pltpu.SemaphoreType.DMA((copies,))],
        compiler_params=pltpu.CompilerParams(vmem_limit_bytes=limit * MIB),
        cost_estimate=COST,
        name=name,
    )(*args)


def softmax(queries, keys, allowed):
    scores = nt(queries, keys) * (HD**-0.5)
    scores = jnp.where(allowed, scores, negative)
    raised = jnp.exp(scores - jnp.max(scores, axis=-1, keepdims=True))
    return raised / jnp.sum(raised, axis=-1, keepdims=True)


def allowed_slots(count):
    row = lax.broadcasted_iota(jnp.int32, (CAP, CAP), 0)
    col = lax.broadcasted_iota(jnp.int32, (CAP, CAP), 1)
    return (col <= row) & (col < count)


def attn_fwd_kernel(
    ids, count_ref, r, s0, s1, s2, s3, n1, qkv, o, part, gate, vec, p_hbm, weights, prob, sem
):
    move = Mover(sem)
    copies = move.weights(ids, (s0, s1, s2, s3), weights)
    w = o.shape[1]
    seqs = r.shape[0] // CAP
    inputs = r[...].astype(F32)
    normal = inputs * lax.rsqrt(jnp.mean(inputs * inputs, axis=-1, keepdims=True) + epsilon)
    wait(copies)
    vectors = weights[:, 4 * w :].astype(F32).T[:8]
    vec[...] = vectors
    n1[...] = (normal * vectors[0:1]).astype(BF)
    logit = jnp.sum(inputs * vectors[2:3], axis=-1, keepdims=True)
    gate[...] = jnp.broadcast_to(jax.nn.sigmoid(logit), gate.shape)
    qkv[...] = nn(n1[...], weights[:, : 3 * w]).astype(BF)
    first = lax.broadcasted_iota(jnp.int32, (CAP, 2 * HD), 1) < HD
    pairs = w // (2 * HD)
    for s in range(seqs):
        allowed = allowed_slots(count_ref[s])
        rows = slice(s * CAP, (s + 1) * CAP)
        for pair in range(pairs):
            at = pair * 2 * HD
            q = qkv[rows, at : at + 2 * HD]
            k = qkv[rows, w + at : w + at + 2 * HD]
            v = qkv[rows, 2 * w + at : 2 * w + at + 2 * HD]
            zero = jnp.zeros_like(q)
            one = softmax(jnp.where(first, q, zero), k, allowed)
            two = softmax(jnp.where(first, zero, q), k, allowed)
            head = 2 * (s * pairs + pair)
            prob[head] = one
            prob[head + 1] = two
            o[rows, at : at + 2 * HD] = jnp.where(first, nn(one.astype(BF), v), nn(two.astype(BF), v)).astype(BF)
        half = pl.ds(2 * s * pairs, 2 * pairs)
        move.put(prob.at[half], p_hbm.at[half])
    part[...] = nt(o[...], weights[:, 3 * w : 4 * w]).astype(BF)
    move.finish()


def attn_fwd(source, counts, routed, w):
    ids, halves = source
    rows, width = routed.shape
    heads = rows // CAP * w // HD
    outs = [
        sds((rows, width), BF), sds((rows, 3 * w), BF), sds((rows, w), BF), sds((rows, width), BF),
        sds((rows, LANE), F32), sds((8, width), F32), sds((FAR * heads, CAP, CAP), F32),
    ]
    return call(
        attn_fwd_kernel, outs, [VM] * 6 + [HB],
        (ids, counts, routed, *halves), [SM, SM, VM] + [ANY] * 4,
        [like((width, 4 * w + EXTRA)), like((heads, CAP, CAP), F32)],
        2 * ids.shape[1] + 4, "attn_fwd", LIMITS[0],
    )


def grad_into(pos, lefts, rights, outs):
    blocks = pos.shape[1]
    width = 2 * outs[0].shape[0]
    rows = width // blocks
    tile = 256
    for at in range(0, width, tile):
        for piece in range(2):
            keep, send = outs[2 * piece], outs[2 * piece + 1]
            col = 0
            for left, right in zip(lefts[piece], rights[piece]):
                value = tn(left[:, at : at + tile], right).astype(BF)
                cols = slice(col, col + right.shape[1])
                col += right.shape[1]
                for b in range(0, tile, rows):
                    place = pos[piece, (at + b) // rows]
                    block = value[b : b + rows]

                    @pl.when(place < blocks // 2)
                    def _():
                        keep[pl.ds(pl.multiple_of(place * rows, rows), rows), cols] = block

                    @pl.when(place >= blocks // 2)
                    def _():
                        send[pl.ds(pl.multiple_of((place - blocks // 2) * rows, rows), rows), cols] = block


def mlp_up_kernel(
    ids, pos, own, other, r, vec, gate, g, s0, s1, s2, s3,
    h_hbm, n2, slope_hbm, z_hbm, dm, k0, d0, k1, d1, h, slope, z, weights, sem,
):
    move = Mover(sem)
    copies = move.weights(ids, (s0, s1, s2, s3), weights)
    h[...] = r[...].astype(F32) + (own[...].astype(F32) + other[...].astype(F32))
    move.put(h, h_hbm)
    normal = h[...] * lax.rsqrt(jnp.mean(h[...] * h[...], axis=-1, keepdims=True) + epsilon)
    n2[...] = (normal * vec[1:2]).astype(BF)
    dm[...] = (gate[:, :1] * g[...].astype(F32)).astype(BF)
    wait(copies)
    a, c = 0.044715, 0.7978845608028654
    step = 512
    for at in range(0, weights.shape[1], step):
        cols = slice(at, at + step)
        u = nn(n2[...], weights[:, cols])
        square = u * u
        t = jnp.tanh(c * (u + a * (square * u)))
        half = 0.5 * (1.0 + t)
        z[:, cols] = (u * half).astype(BF)
        slope[:, cols] = half + 0.5 * u * (1.0 - t * t) * (c * (1.0 + 3.0 * a * square))
        move.put(slope.at[:, pl.ds(at, step)], slope_hbm.at[pl.ds(0, slope.shape[0]), pl.ds(at, step)])
    move.put(z, z_hbm)
    cut = k0.shape[1]
    grad_into(pos, [[dm], [dm]], [[z[:, :cut]], [z[:, cut:]]], (k0, d0, k1, d1))
    move.finish()


def places_of(width, n):
    if (width // n) % 16 == 0:
        return jnp.stack([places(n, o) for o in color_orders(n)])
    return jnp.zeros((2, 16), jnp.int32) + jnp.arange(16, dtype=jnp.int32)


def grad_shapes(width, total):
    cut = split_of(total)
    return [sds((width // 2, c), BF) for c in (cut, cut, total - cut, total - cut)]


def scatter_of(outs, width, n):
    keep0, send0, keep1, send1 = outs
    keep, send = [keep0, keep1], [send0, send1]
    if (width // n) % 16:
        orders = color_orders(n)
        for at in range(2):
            whole = jnp.concatenate([keep[at], send[at]], axis=0).reshape(n, width // n, -1)
            whole = whole[owners(n, orders[at])].reshape(width, -1)
            keep[at], send[at] = whole[: width // 2], whole[width // 2 :]
    return Scatter(keep, send, n)


def mlp_up(source, pos, own, other, routed, upstream, gate, vec, hidden, n):
    ids, halves = source
    rows, width = routed.shape
    outs = [
        sds((rows, width), F32), sds((rows, width), BF), sds((FAR * rows, hidden), F32),
        sds((rows, hidden), BF), sds((rows, width), BF),
    ]
    result = call(
        mlp_up_kernel, outs + grad_shapes(width, hidden), [HB, VM, HB, HB, VM] + [VM] * 4,
        (ids, pos, own, other, routed, vec, gate, upstream, *halves), [SM] * 2 + [VM] * 6 + [ANY] * 4,
        [like((rows, width), F32), like((rows, hidden), F32), like((rows, hidden)), like((width, hidden))],
        2 * ids.shape[1] + 16, "mlp_up", LIMITS[1],
    )
    return result[:5], scatter_of(result[5:], width, n)


def mlp_back_kernel(
    idu, idd, dm, slope_hbm, u0, u1, u2, u3, d0, d1, d2, d3, du, part, slope, wu, wd, sem
):
    move = Mover(sem)
    step = 512
    down = move.weights(idd, (d0, d1, d2, d3), wd)
    tiles = [
        move.start(slope_hbm.at[pl.ds(0, slope.shape[0]), pl.ds(at, step)], slope.at[:, pl.ds(at, step)])
        for at in range(0, wd.shape[1], step)
    ]
    up = move.weights(idu, (u0, u1, u2, u3), wu)
    wait(down)
    for at in range(0, wd.shape[1], step):
        dz = nn(dm[...], wd[:, at : at + step])
        tiles[at // step].wait()
        du[:, at : at + step] = (dz * slope[:, at : at + step]).astype(BF)
    wait(up)
    part[...] = nt(du[...], wu[...]).astype(BF)


def mlp_back(up, down, dm, slope):
    rows, width = dm.shape
    hidden = slope.shape[1]
    return call(
        mlp_back_kernel, [sds((rows, hidden), BF), sds((rows, width), BF)], [VM, VM],
        (up[0], down[0], dm, slope, *up[1], *down[1]), [SM, SM, VM, HB] + [ANY] * 8,
        [like((rows, hidden), F32)] + [like((width, hidden))] * 2,
        4 * up[0].shape[1] + 8, "mlp_back", LIMITS[2],
    )


def grad_up_kernel(pos, n2, du, k0, d0, k1, d1, sem):
    cut = k0.shape[1]
    grad_into(pos, [[n2], [n2]], [[du[:, :cut]], [du[:, cut:]]], (k0, d0, k1, d1))


def grad_up(pos, n2, du, n):
    width = n2.shape[1]
    hidden = du.shape[1]
    result = call(
        grad_up_kernel, grad_shapes(width, hidden), [VM] * 4,
        (pos, n2, du), [SM, VM, VM], [], 1, "grad_up", LIMITS[3],
    )
    return scatter_of(result, width, n)


def mlp_out_kernel(idd, dn1, z_hbm, d0, d1, d2, d3, both, z, wd, sem):
    move = Mover(sem)
    first = move.start(z_hbm, z)
    copies = move.weights(idd, (d0, d1, d2, d3), wd)
    rows = dn1.shape[0]
    both[rows:] = dn1[...]
    wait(copies)
    first.wait()
    both[:rows] = nt(z[...], wd[...]).astype(BF)


def mlp_out(down, z, dn1):
    rows, hidden = z.shape
    width = dn1.shape[1]
    return call(
        mlp_out_kernel, sds((2 * rows, width), BF), VM,
        (down[0], dn1, z, *down[1]), [SM, VM, HB] + [ANY] * 4,
        [like((rows, hidden)), like((width, hidden))],
        2 * down[0].shape[1] + 8, "mlp_out", LIMITS[4],
    )


def attn_back_kernel(
    ids, pos, own, other, vec, gate, g, qkv, n1, o, h_hbm, p_hbm, s0, s1, s2, s3,
    dh_hbm, part, gain_out, k0, d0, k1, d1, h, prob, dh, weights, da, do_ref, dqkv, sem,
):
    move = Mover(sem)
    early = move.start(h_hbm, h)
    copies = move.weights(ids, (s0, s1, s2, s3), weights)
    heads_in = move.start(p_hbm.at[pl.ds(0, prob.shape[0])], prob)
    rows = h.shape[0]
    w = do_ref.shape[1]
    dn2 = own[rows:].astype(F32) + other[rows:].astype(F32)
    early.wait()
    inverse = lax.rsqrt(jnp.mean(h[...] * h[...], axis=-1, keepdims=True) + epsilon)
    normal = h[...] * inverse
    product = dn2 * normal
    gain_out[...] = jnp.broadcast_to(jnp.sum(product, axis=0, keepdims=True), gain_out.shape)
    gain = vec[1:2]
    dh[...] = inverse * (dn2 * gain - normal * jnp.mean(product * gain, axis=-1, keepdims=True))
    move.put(dh, dh_hbm)
    da[...] = (gate[:, :1] * g[...].astype(F32) + dh[...]).astype(BF)
    wait(copies)
    do_ref[...] = nn(da[...], weights[:, 3 * w : 4 * w]).astype(BF)
    heads_in.wait()
    first = lax.broadcasted_iota(jnp.int32, (CAP, 2 * HD), 1) < HD
    scale = HD**-0.5
    pairs = w // (2 * HD)
    for s in range(rows // CAP):
        at_rows = slice(s * CAP, (s + 1) * CAP)
        for pair in range(pairs):
            at = pair * 2 * HD
            q = qkv[at_rows, at : at + 2 * HD]
            k = qkv[at_rows, w + at : w + at + 2 * HD]
            v = qkv[at_rows, 2 * w + at : 2 * w + at + 2 * HD]
            do = do_ref[at_rows, at : at + 2 * HD]
            zero = jnp.zeros_like(q)
            results = []
            for head in range(2):
                do_one = jnp.where(first, do, zero) if head == 0 else jnp.where(first, zero, do)
                probability = prob[2 * (s * pairs + pair) + head]
                d_probability = nt(do_one, v)
                dv = tn(probability.astype(BF), do)
                inner = jnp.sum(probability * d_probability, axis=-1, keepdims=True)
                ds = (probability * (d_probability - inner)).astype(BF)
                results.append((nn(ds, k) * scale, tn(ds, q) * scale, dv))
            for which in range(3):
                value = jnp.where(first, results[0][which], results[1][which]).astype(BF)
                dqkv[at_rows, which * w + at : which * w + at + 2 * HD] = value
    cut = k0.shape[1]
    grad_into(pos, [[n1], [n1, da]], [[dqkv[:, :cut]], [dqkv[:, cut:], o[...]]], (k0, d0, k1, d1))
    part[...] = nt(dqkv[...], weights[:, : 3 * w]).astype(BF)
    move.finish()


def attn_back(source, pos, own, other, h, vec, upstream, gate, qkv, prob, n1, attended, n):
    ids, halves = source
    rows, width = h.shape
    w = attended.shape[1]
    outs = [sds((rows, width), F32), sds((rows, width), BF), sds((8, width), F32)]
    result = call(
        attn_back_kernel, outs + grad_shapes(width, 4 * w), [HB, VM, VM] + [VM] * 4,
        (ids, pos, own, other, vec, gate, upstream, qkv, n1, attended, h, prob, *halves),
        [SM] * 2 + [VM] * 8 + [HB] * 2 + [ANY] * 4,
        [
            like((rows, width), F32), like((prob.shape[0] // FAR, CAP, CAP), F32), like((rows, width), F32),
            like((width, 4 * w + EXTRA)), like((rows, width)), like((rows, w)), like((rows, 3 * w)),
        ],
        2 * ids.shape[1] + 8, "attn_back", LIMITS[5],
    )
    return result[:3], scatter_of(result[3:], width, n)


TILE = 1024


def select_rows(slot_ref, sel, rows, x_ref, out_ref):
    place = lax.broadcasted_iota(jnp.int32, (CAP, LANE), 0).astype(F32)
    for at in range(TILE // LANE):
        sel[:, at * LANE : (at + 1) * LANE] = jnp.where(place == slot_ref[at], 1.0, 0.0).astype(BF)
    put = tn(sel[...], rows[...])
    hit = tn(sel[...], jnp.ones((CAP, LANE), BF))[:, :1]
    out_ref[...] = jnp.where(hit > 0.5, put.astype(BF), x_ref[...])


def place_kernel(slot_ref, x_ref, rows, out_ref, sel):
    select_rows(slot_ref, sel, rows, x_ref, out_ref)


def place_rows(slot, tokens, rows, name):
    width = tokens.shape[1]
    per = LEN // TILE
    seqs = tokens.shape[0] // LEN
    groups = TILE // LANE
    return pl.pallas_call(
        place_kernel,
        grid=(seqs, per),
        in_specs=[
            pl.BlockSpec((groups, 1, LANE), lambda s, t: (s * per + t, 0, 0)),
            pl.BlockSpec((TILE, width), lambda s, t: (s * per + t, 0)),
            pl.BlockSpec((CAP, width), lambda s, t: (s, 0)),
        ],
        out_specs=pl.BlockSpec((TILE, width), lambda s, t: (s * per + t, 0)),
        out_shape=sds(tokens.shape, BF),
        scratch_shapes=[pltpu.VMEM((CAP, TILE), BF)],
        compiler_params=pltpu.CompilerParams(vmem_limit_bytes=LIMITS[6] * MIB),
        cost_estimate=COST,
        name=name,
    )(slot, tokens, rows)


def rows_kernel(
    count_ref, both_own, both_other, dn1_own, dn1_other, attn_own_any, attn_other_any, r_any, g_any, gate_any, vec_any, dh_any,
    out_ref, back_ref, small_ref, attn_own, attn_other, r, g, gate_ref, vec, dh, sem,
):
    move = Mover(sem)
    pairs = (
        (r_any, r), (g_any, g), (attn_own_any, attn_own), (attn_other_any, attn_other),
        (gate_any, gate_ref), (vec_any, vec), (dh_any, dh),
    )
    copies = [move.start(src, dst) for src, dst in pairs]
    rows = r.shape[0]
    wait(copies)
    inputs = r[...].astype(F32)
    upstream = g[...].astype(F32)
    gate = gate_ref[:, :1]
    attention = attn_own[...].astype(F32) + attn_other[...].astype(F32)
    branch = attention + (both_own[:rows].astype(F32) + both_other[:rows].astype(F32))
    out_ref[...] = (inputs + gate * branch).astype(BF)
    dl = jnp.sum(upstream * branch, axis=-1, keepdims=True) * gate * (1.0 - gate)
    d_router = jnp.sum(dl * inputs, axis=0, keepdims=True)
    dn1 = dn1_own[...].astype(F32) + dn1_other[...].astype(F32)
    inverse = lax.rsqrt(jnp.mean(inputs * inputs, axis=-1, keepdims=True) + epsilon)
    normal = inputs * inverse
    product = dn1 * normal
    d_gain = jnp.sum(product, axis=0, keepdims=True)
    gain = vec[0:1]
    dr = inverse * (dn1 * gain - normal * jnp.mean(product * gain, axis=-1, keepdims=True))
    back_ref[...] = (upstream + dh[...] + dl * vec[2:3] + dr).astype(BF)
    row = lax.broadcasted_iota(jnp.int32, (CAP, LANE), 0)
    total = jnp.zeros((1, LANE), F32)
    for s in range(rows // CAP):
        part = gate_ref[s * CAP : (s + 1) * CAP]
        total += jnp.sum(jnp.where(row < count_ref[s], part, 0.0), axis=0, keepdims=True)
    small_ref[0:1] = d_gain
    small_ref[1:2] = d_router
    small_ref[2:3] = jnp.concatenate([total] * (d_gain.shape[1] // LANE), axis=1)
    small_ref[3:8] = jnp.zeros((5, d_gain.shape[1]), F32)


def rows_last(counts, attn_own, attn_other, both_own, both_other, dn1_own, dn1_other, routed, upstream, gate, vec, dh):
    rows, width = routed.shape
    ins = (attn_own, attn_other, routed, upstream, gate, vec, dh)
    return call(
        rows_kernel,
        [sds((rows, width), BF), sds((rows, width), BF), sds((8, width), F32)], [VM] * 3,
        (counts, both_own, both_other, dn1_own, dn1_other, *ins), [SM] + [VM] * 4 + [ANY] * len(ins),
        [like(x.shape, x.dtype) for x in ins], len(ins), "rows_last", LIMITS[8],
    )


def body(
    tokens_in,
    route_mask,
    cotangent,
    w_query,
    w_key,
    w_value,
    w_out,
    w_up,
    w_down,
    gain_attn,
    gain_mlp,
    router,
):
    n = lax.axis_size("dp")
    mine, w = w_query.shape
    hidden = w_up.shape[1]
    width = tokens_in.shape[1]
    seqs = tokens_in.shape[0] // LEN
    extras = jnp.concatenate(
        [gain_attn[:, None], gain_mlp[:, None], router[:, None], jnp.zeros((mine, EXTRA - 3), BF)], axis=1
    )
    attn = Gather(jnp.concatenate([w_query, w_key, w_value, w_out.T, extras], axis=1), n)
    up = Gather(w_up, n)
    down = Gather(w_down.T, n)
    counts = jnp.sum(route_mask.reshape(seqs, LEN), axis=1).astype(jnp.int32)

    def start(chains, token, swaps=()):
        held = [c.held if isinstance(c, Gather) else c.send for c in chains]
        flat = tie([v for h in held for v in h] + list(swaps), token)
        arrived = []
        for chain, h in zip(chains, held):
            part, flat = flat[: len(h)], flat[len(h) :]
            if isinstance(chain, Gather):
                chain.held = part
            else:
                chain.send = part
            arrived += chain.begin()
        swapped = [other_core(v) for v in flat]
        return arrived + swapped, swapped

    def close(chains, made=()):
        flat = tie([g for c in chains for g in c.got], made)
        for chain in chains:
            chain.got, flat = flat[: len(chain.got)], flat[len(chain.got) :]
            chain.end()

    pos = places_of(width, n)
    four = attn.steps == 4

    token, _ = start([attn], [])
    routed, upstream, slot = pick(route_mask, tokens_in, cotangent, seqs)
    close([attn], [slot])
    for chains in ([attn, up], [attn, up], [attn, down]) if four else [[attn, up, down]] * (attn.steps - 1):
        token, _ = start(chains, token)
        close(chains)
    src_attn = attn.result()
    rest = [[up, down], [up, down], [down]] if four else [[up, down], [], []]
    token, _ = start(rest[0], token)
    n1, qkv, attended, attn_own, gate, vec, prob = attn_fwd(src_attn, counts, routed, w)
    close(rest[0], [attn_own])
    token, (attn_other,) = start(rest[1], token, [attn_own])
    close(rest[1])
    src_up = up.result()
    token, _ = start(rest[2], token)
    (h, n2, slope, z, dm), sum_down = mlp_up(
        src_up, pos, attn_own, attn_other, routed, upstream, gate, vec, hidden, n
    )
    close(rest[2], [dm])
    src_down = down.result()

    token, _ = start([sum_down], token)
    du, dn2_own = mlp_back(src_up, src_down, dm, slope)
    both_own = mlp_out(src_down, z, dn2_own)
    sum_up = grad_up(pos, n2, du, n)
    close([sum_down], sum_up.send + [both_own])
    token, (both_other,) = start([sum_up, sum_down], token, [both_own])
    (dh, dn1_own, gain_two), sum_attn = attn_back(
        src_attn, pos, both_own, both_other, h, vec, upstream, gate, qkv, prob, n1, attended, n
    )
    close([sum_up, sum_down], [gain_two])
    token, (dn1_other,) = start([sum_attn, sum_down], token, [dn1_own])
    down_there = token[-3:-1]
    close([sum_down])
    more, _ = start([sum_up], down_there)
    out_rows, back_rows, sums = rows_last(
        counts, attn_own, attn_other, both_own, both_other, dn1_own, dn1_other, routed, upstream, gate, vec, dh
    )
    block_out = place_rows(slot, tokens_in, out_rows, "place_out")
    close([sum_attn, sum_up], [block_out])
    token = token + more
    token, _ = start([sum_attn, sum_up, sum_down], token)
    (back_late,) = tie([back_rows], [token[3]])
    input_grad = place_rows(slot, cotangent, back_late, "place_grad")
    close([sum_attn, sum_up, sum_down], [input_grad])
    live = [c for c in (sum_attn, sum_up, sum_down) if c.at]
    sum_attn.apart = True
    first = True
    while live:
        token, _ = start(live, token)
        if first:
            first = False
            sums, gain_two = tie([sums, gain_two], [token[0]])
            scalars = jnp.where(jnp.arange(width) % mine == 0, jnp.sum(counts).astype(F32), sums[2])
            small = jnp.stack([sums[0], gain_two[0], sums[1], scalars])
            small = small.reshape(4, n, mine).transpose(1, 0, 2).reshape(n, 4 * mine)
        if len(live) == 1 and live[0].at == 0:
            (small,) = tie([small], [token[-1]])
            small = lax.all_to_all(small, "dp", 0, 0, tiled=True)
        close(live)
        live = [c for c in live if c.at]
    small = jnp.sum(small, axis=0)
    total_attn, total_up, total_down = sum_attn.result(), sum_up.result(), sum_down.result()
    token_total = tokens_in.shape[0] * n
    return (
        block_out,
        input_grad,
        total_attn[:, :w],
        total_attn[:, w : 2 * w],
        total_attn[:, 2 * w : 3 * w],
        total_attn[:, 3 * w :].T,
        total_up,
        total_down.T,
        small[:mine],
        small[mine : 2 * mine],
        small[2 * mine : 3 * mine],
        small[3 * mine] / token_total,
        small[3 * mine + 1] / small[3 * mine],
    )


def solution(mesh):
    rows, cols = P("dp", "mp"), P("mp", "dp")
    return jax.shard_map(
        body,
        mesh=mesh,
        in_specs=(P("dp", None), P("dp"), P("dp", None), rows, rows, rows, cols, rows, cols) + (P("dp"),) * 3,
        out_specs=(P("dp", None), P("dp", None), rows, rows, rows, cols, rows, cols) + (P("dp"),) * 3 + (P(), P()),
        check_vma=False,
    )
```
